32 devices in a mesh: bead: 8 (over z, x), space: 4 (over y, core).
Axes of the slice: x: 2, y: 2, z: 4, core: 2. Of those that a mesh axis runs over, the one named last changes fastest.
Arguments:
- positions: float32 [64, 3, 1024], P('bead', None, 'space'), may hold values from -1 to 5
- species: int32 [1024], P('space'), may hold values from 0 to 1
- neighbors: int32 [32, 1024], P(None, 'space'), may hold values from 0 to 383, as said below
- counts: int32 [1024], P('space'), may hold values from 1 to 32, as said below
- send_rows: int32 [512], P('space'), may hold values from 0 to 255, as said below
- embed: float32 [2, 128], replicated, may hold values from -6 to 6
- w_radial: float32 [2, 8, 128], replicated, may hold values from -2 to 2
- w_msg: float32 [2, 128, 128], replicated, may hold values from -0.5 to 0.5
- w_upd: float32 [2, 128, 128], replicated, may hold values from -0.5 to 0.5
- w_out: float32 [128], replicated, may hold values from -0.5 to 0.5
Outputs:
- forces: float32 [64, 3, 1024], P('bead', None, 'space')
The draws below stay inside these ranges and needn't reach their ends.
Inputs may be any that keep to these rules, and one draw needn't show every extreme that they name: `neighbors`: entry n < 256 is the domain's own row n; 256 + s is the s-th left ghost and 320 + s the s-th right ghost. `counts`: slots of an atom below its count are live, the others padding. `send_rows`: each domain's first 64 entries are a permutation of its rows 0 to 63, the next 64 a permutation of its rows 192 to 255.
All inputs are finite; a program needn't handle non-finite values.
Results may differ from the reference program's by a relative error of at most 0.0003.
Values sent between devices are 32-bit elements; how exact they have to be, the bound alone decides.
No kernel may reach another device: no remote copies, remote signals or barrier semaphores. Data moves between devices by JAX's collectives and lax.ppermute only.
A program may use at most 64 MiB of HBM per device.

```python
import jax
import jax.numpy as jnp
from jax import lax

P_SIZE = 64
PC = 16
CH = 128
NB = 8
SPECIES = 2
K = 32
LAYERS = 2
A_DEV = 256
GH = 64
NATOMS = 1024
N_SPACE = 4


def draw_positions(key, part):
    first_key, second_key, third_key = jax.random.split(jax.random.fold_in(key, 11), 3)
    atom_index = jnp.arange(NATOMS, dtype=jnp.int32)
    domain = (atom_index // A_DEV).astype(jnp.float32)
    within = (atom_index % A_DEV).astype(jnp.float32)
    jitter = jax.random.uniform(first_key, (NATOMS,), jnp.float32)
    across = jax.random.uniform(second_key, (2, NATOMS), jnp.float32)
    centre = jnp.concatenate([(domain + (within + jitter) / A_DEV)[None], across], axis=0)
    spread = 0.05 * jnp.clip(jax.random.normal(third_key, (P_SIZE, 3, NATOMS), jnp.float32), -6.0, 6.0)
    return (centre[None] + spread).astype(jnp.float32)


def draw_neighbors(key, part):
    domains = NATOMS // A_DEV
    first_key, second_key, third_key, fourth_key = jax.random.split(jax.random.fold_in(key, 23), 4)
    shape_now = (K, domains, A_DEV)
    stride = jax.random.randint(first_key, shape_now, 1, GH + 1)
    direction = jax.random.randint(second_key, shape_now, 0, 2) * 2 - 1
    target = jnp.arange(A_DEV, dtype=jnp.int32)[None, None, :] + stride * direction
    left_slot = A_DEV + jax.random.randint(third_key, shape_now, 0, GH)
    right_slot = A_DEV + GH + jax.random.randint(fourth_key, shape_now, 0, GH)
    picked = jnp.where(target < 0, left_slot, jnp.where(target >= A_DEV, right_slot, target))
    return picked.reshape(K, NATOMS).astype(jnp.int32)


def draw_counts(key, part):
    domains = NATOMS // A_DEV
    first_key, second_key, third_key = jax.random.split(jax.random.fold_in(key, 37), 3)
    ceilings = jax.random.randint(first_key, (domains,), K // 4, K + 1)
    heaviest = jax.random.randint(second_key, (), 0, domains)
    ceilings = jnp.where(jnp.arange(domains, dtype=jnp.int32) == heaviest, K, ceilings)
    spread = jax.random.randint(third_key, (domains, A_DEV), 0, K)
    result = 1 + spread % ceilings[:, None]
    result = result.at[:, 0].set(ceilings)
    return result.reshape(NATOMS).astype(jnp.int32)


def draw_send_rows(key, part):
    domains = NATOMS // A_DEV
    first_key, second_key = jax.random.split(jax.random.fold_in(key, 53), 2)
    left_perm = jax.vmap(lambda sub_key: jax.random.permutation(sub_key, GH))(jax.random.split(first_key, domains))
    right_perm = jax.vmap(lambda sub_key: jax.random.permutation(sub_key, GH))(jax.random.split(second_key, domains))
    both_sides = jnp.concatenate([left_perm, A_DEV - GH + right_perm], axis=1)
    return both_sides.reshape(2 * GH * domains).astype(jnp.int32)


def place_ends(drawn, own_key, low, high):
    longest = drawn.shape.index(max(drawn.shape))
    spots = []
    for shift in (0, 1):
        where = [jax.random.randint(jax.random.fold_in(own_key, axis), (), 0, length) for axis, length in enumerate(drawn.shape)]
        where[longest] = (where[longest] + shift) % drawn.shape[longest]
        spots.append(tuple(where))
    return drawn.at[spots[0]].set(low).at[spots[1]].set(high)


def centred(own_key, dims, deviation, limit, held_as=jnp.bfloat16):
    return jnp.clip(deviation * jax.random.normal(own_key, dims, jnp.float32), -limit, limit).astype(held_as)


def setup_inputs(seed: int = 0) -> dict:
    key_of = jax.random.split(jax.random.key(seed), 11)
    return {
        "positions": draw_positions(jax.random.fold_in(key_of[10], 71), 0),
        "species": place_ends(jax.random.randint(key_of[1], (NATOMS,), 0, SPECIES), jax.random.fold_in(key_of[1], 1), 0, SPECIES - 1).astype(jnp.int32),
        "neighbors": draw_neighbors(jax.random.fold_in(key_of[10], 71), 0),
        "counts": draw_counts(jax.random.fold_in(key_of[10], 71), 0),
        "send_rows": draw_send_rows(jax.random.fold_in(key_of[10], 71), 0),
        "embed": centred(key_of[5], (SPECIES, CH), 1.0, 6.0, jnp.float32),
        "w_radial": centred(key_of[6], (LAYERS, NB, CH), NB ** -0.5, 2.0, jnp.float32),
        "w_msg": centred(key_of[7], (LAYERS, CH, CH), CH ** -0.5, 0.5, jnp.float32),
        "w_upd": centred(key_of[8], (LAYERS, CH, CH), CH ** -0.5, 0.5, jnp.float32),
        "w_out": centred(key_of[9], (CH,), CH ** -0.5, 0.5, jnp.float32),
    }


exact_mode = lax.Precision.HIGHEST
spacing_floor = 0.01
radial_width = 0.2
radial_reach = 1.5

def contraction(full_beads, reduced_beads):
    rowpos = jnp.arange(reduced_beads, dtype=jnp.float32)[:, None]
    colpos = jnp.arange(full_beads, dtype=jnp.float32)[None, :]
    phase_gap = rowpos / reduced_beads - colpos / full_beads
    running = jnp.ones_like(phase_gap)
    for harmonic in range(1, reduced_beads // 2):
        running = running + 2.0 * jnp.cos(2.0 * jnp.pi * harmonic * phase_gap)
    running = running + jnp.cos(jnp.pi * reduced_beads * phase_gap)
    return running / full_beads

def extend(stacked, sends):
    lent_pack = jax.vmap(lambda values, chosen: values[chosen])(stacked, sends)
    from_left = jnp.roll(lent_pack, 1, axis=0)[:, GH:]
    from_right = jnp.roll(lent_pack, -1, axis=0)[:, :GH]
    return jnp.concatenate([stacked, from_left, from_right], axis=1)

def bead_energy(points, onehot, neighbor_rows, live_slots, sends, embed, w_radial, w_msg, w_upd, w_out):
    extended = extend(points, sends)
    domain = jnp.arange(N_SPACE, dtype=jnp.int32)[:, None]
    rowidx = jnp.arange(A_DEV + 2 * GH, dtype=jnp.int32)[None, :]
    raised = ((domain == N_SPACE - 1) & (rowidx >= A_DEV + GH)).astype(jnp.float32)
    lowered = ((domain == 0) & (rowidx >= A_DEV) & (rowidx < A_DEV + GH)).astype(jnp.float32)
    extended = extended.at[:, :, 0].add(N_SPACE * (raised - lowered))
    near_points = jax.vmap(lambda values, chosen: values[chosen])(extended, neighbor_rows)
    displace = near_points - points[:, None]
    distance = jnp.sqrt(lax.optimization_barrier(jnp.sum(displace * displace, axis=-1)) + spacing_floor)
    centers = radial_reach * jnp.arange(NB, dtype=jnp.float32) / (NB - 1)
    offsets = (distance[..., None] - centers) / radial_width
    radial_basis = jnp.exp(-offsets * offsets)
    edge_scale = K ** (-0.5)
    hidden = jnp.einsum('sat,tc->sac', onehot, embed, precision=exact_mode)
    for layer_index in range(LAYERS):
        lent = jnp.einsum('sac,cd->sad', hidden, w_msg[layer_index], precision=exact_mode)
        lent_ext = extend(lent, sends)
        radial_w = jnp.einsum('skan,nc->skac', radial_basis, w_radial[layer_index], precision=exact_mode)
        near_rows = jax.vmap(lambda values, chosen: values[chosen])(lent_ext, neighbor_rows)
        message = edge_scale * lax.optimization_barrier(jnp.sum(live_slots[..., None] * radial_w * near_rows, axis=1))
        update = jnp.einsum('sac,cd->sad', message, w_upd[layer_index], precision=exact_mode)
        hidden = hidden + jax.nn.silu(update)
    return jnp.sum(hidden * w_out)

def reference(positions, species, neighbors, counts, send_rows, embed, w_radial, w_msg, w_upd, w_out):
    contract_table = contraction(P_SIZE, PC)
    reduced = jnp.einsum('kj,jcn->kcn', contract_table, positions, precision=exact_mode)
    points = reduced.reshape(PC, 3, N_SPACE, A_DEV).transpose(0, 2, 3, 1)
    onehot = (species.reshape(N_SPACE, A_DEV)[..., None] == jnp.arange(SPECIES, dtype=jnp.int32)).astype(jnp.float32)
    neighbor_rows = neighbors.reshape(K, N_SPACE, A_DEV).transpose(1, 0, 2)
    live_slots = (jnp.arange(K, dtype=jnp.int32)[None, :, None] < counts.reshape(N_SPACE, 1, A_DEV)).astype(jnp.float32)
    sends = send_rows.reshape(N_SPACE, 2 * GH)

    def one_bead(bead_points):
        slope = jax.grad(bead_energy)(bead_points, onehot, neighbor_rows, live_slots, sends, embed, w_radial, w_msg, w_upd, w_out)
        return -slope
    pulled = lax.map(one_bead, points)
    pulled = pulled.transpose(0, 3, 1, 2).reshape(PC, 3, NATOMS)
    return float(P_SIZE) / PC * jnp.einsum('kj,kcn->jcn', contract_table, pulled, precision=exact_mode)
```

```python
import functools
import math

import jax
import jax.numpy as jnp
import numpy as np
from jax import lax
from jax.experimental import pallas as pl
from jax.experimental.pallas import tpu as pltpu
from jax.sharding import PartitionSpec as P

PC = 16

exact_mode = lax.Precision.HIGHEST
spacing_floor = 0.01
radial_width = 0.2
radial_reach = 1.5
LANES = 128
PLANES = 4
ROWS = 16
BLOCK = 64
F32 = jnp.float32
BF16 = jnp.bfloat16
VMEM_BYTES = 48 * 1024 * 1024
kappa = math.sqrt(math.log2(math.e)) / radial_width


def contraction(full_beads, reduced_beads):
    gap = np.arange(reduced_beads)[:, None] / reduced_beads - np.arange(full_beads)[None, :] / full_beads
    total = np.ones_like(gap)
    for harmonic in range(1, reduced_beads // 2):
        total = total + 2.0 * np.cos(2.0 * np.pi * harmonic * gap)
    total = total + np.cos(np.pi * reduced_beads * gap)
    return (total / full_beads).astype(np.float32)


def exact_dot(left, right):
    return lax.dot(left, right, precision=exact_mode, preferred_element_type=F32)


def fast_dot(left, right):
    return lax.dot(left, right, preferred_element_type=F32)


def halves(values):
    high = values.astype(BF16)
    low = (values - high.astype(F32)).astype(BF16)
    return high, low


def spread_kernel(table_ref, pos_ref, out_ref):
    full_dev = pos_ref.shape[0]
    groups, domains, rows, _ = out_ref.shape
    first = lax.axis_index("bead") * full_dev
    beads = [pos_ref[j] for j in range(full_dev)]
    for group in range(groups):
        for local in range(rows // 3):
            k = group * (rows // 3) + local
            total = table_ref[k, first] * beads[0]
            for j in range(1, full_dev):
                total = total + table_ref[k, first + j] * beads[j]
            for domain in range(domains):
                out_ref[group, domain, local * 3 : local * 3 + 3, :] = total


def collect_kernel(ratio, table_ref, in_ref, out_ref):
    full_dev = out_ref.shape[0]
    groups, domains, rows, _ = in_ref.shape
    first = lax.axis_index("bead") * full_dev
    totals = [None] * full_dev
    for group in range(groups):
        arrived = in_ref[group, 0]
        for domain in range(1, domains):
            arrived = arrived + in_ref[group, domain]
        for local in range(rows // 3):
            k = group * (rows // 3) + local
            part = arrived[local * 3 : local * 3 + 3, :] * -ratio
            for j in range(full_dev):
                term = table_ref[k, first + j] * part
                totals[j] = term if totals[j] is None else totals[j] + term
    for j in range(full_dev):
        out_ref[j] = totals[j]


def prepare_kernel(
    own_ref, left_ref, right_ref, far_left_ref, far_right_ref, embed_ref, radial_ref, msg_ref, upd_ref,
    count_ref, hidden_ref, first_ref, first_t_ref, msg_t_ref, upd_t_ref,
    *, slots, ghosts,
):
    atoms = own_ref.shape[1]
    extent = atoms + 2 * ghosts
    species_count, channels = embed_ref.shape
    basis_count = radial_ref.shape[1]
    tail = atoms - ghosts
    count_row, species_row, send_row = slots, slots + 1, slots + 2

    def edge_pack(row, rows=1):
        return jnp.concatenate(
            [own_ref[row : row + rows], left_ref[row : row + rows, tail:], right_ref[row : row + rows, :ghosts]],
            axis=1,
        )

    neighbors = edge_pack(0, slots)
    counts = edge_pack(count_row)
    own_send = own_ref[send_row : send_row + 1]
    left_send = left_ref[send_row : send_row + 1]
    right_send = right_ref[send_row : send_row + 1]
    far_left_send = far_left_ref[1:2]
    far_right_send = far_right_ref[1:2]

    def ghost_map(from_left, from_right):
        return jnp.concatenate(
            [from_left[:, ghosts : 2 * ghosts] - tail, from_right[:, :ghosts] + ghosts], axis=1
        )

    maps = [
        ghost_map(left_send, right_send),
        ghost_map(far_left_send, own_send),
        ghost_map(own_send, far_right_send),
    ]
    maps = [jnp.broadcast_to(m, (slots, 2 * ghosts)) for m in maps]
    lane = lax.broadcasted_iota(jnp.int32, (slots, LANES), 1)
    slot = lax.broadcasted_iota(jnp.int32, (slots, LANES), 0)

    species_rows = []
    for near, lower, upper in (
        (own_ref[species_row : species_row + 1], left_ref[species_row : species_row + 1], right_ref[species_row : species_row + 1]),
        (left_ref[species_row : species_row + 1], far_left_ref[0:1], own_ref[species_row : species_row + 1]),
        (right_ref[species_row : species_row + 1], own_ref[species_row : species_row + 1], far_right_ref[0:1]),
    ):
        species_rows.append(jnp.concatenate([near, lower[:, tail:], upper[:, :ghosts]], axis=1))
    species_f = jnp.concatenate(species_rows + [species_rows[0]] * 5, axis=0).astype(F32)
    species_cols = species_f.T

    plane_rows = extent // PLANES
    chunks = extent // LANES
    plane_iota = lax.broadcasted_iota(jnp.int32, (plane_rows, LANES), 0)
    lane_block = lax.broadcasted_iota(jnp.int32, (plane_rows, LANES), 1)
    for chunk in range(chunks):
        lanes = slice(chunk * LANES, (chunk + 1) * LANES)
        rows_now = neighbors[:, lanes]
        index = jnp.clip(rows_now - atoms, 0, 2 * ghosts - 1)
        if (chunk + 1) * LANES <= atoms:
            mapped = jnp.take_along_axis(maps[0], index, axis=1, mode="promise_in_bounds")
        else:
            mapped = jnp.where(
                lane < ghosts,
                jnp.take_along_axis(maps[1], index, axis=1, mode="promise_in_bounds"),
                jnp.take_along_axis(maps[2], index, axis=1, mode="promise_in_bounds"),
            )
        rows_now = jnp.where(rows_now >= atoms, atoms + mapped, rows_now)
        plane = jnp.zeros_like(rows_now)
        for step in range(1, PLANES):
            plane = plane + (rows_now >= step * plane_rows).astype(jnp.int32)
        within = rows_now - plane * plane_rows
        within = jnp.where(slot < counts[:, lanes], within, -1)
        value = jnp.left_shift(jnp.ones_like(plane), 8 * plane)
        words = jnp.zeros((plane_rows, LANES), jnp.int32)
        for k in range(slots):
            words = words + jnp.where(within[k : k + 1] == plane_iota, value[k : k + 1], 0)
        for step in range(PLANES):
            rows = slice(step * plane_rows, (step + 1) * plane_rows)
            tally = (jnp.right_shift(words, 8 * step) & 255).astype(F32)
            if (chunk + 1) * LANES <= atoms:
                kind = jnp.broadcast_to(species_cols[rows, 0:1], (plane_rows, LANES))
            else:
                kind = jnp.where(lane_block < ghosts, species_cols[rows, 1:2], species_cols[rows, 2:3])
            for s in range(species_count):
                count_ref[s, rows, lanes] = jnp.where(kind == float(s), tally, 0.0)

    embed = embed_ref[...]
    embed_pad = jnp.concatenate([embed, jnp.zeros((8 - species_count, channels), F32)], axis=0)
    embed_cols = embed_pad.T
    hidden = jnp.zeros((channels, extent), F32)
    for s in range(species_count):
        hidden = hidden + embed_cols[:, s : s + 1] * (species_f[0:1] == float(s)).astype(F32)
    hidden_ref[...] = hidden

    scale = slots ** (-0.5)
    lent = exact_dot(embed_pad, msg_ref[0])
    stacked = []
    for b in range(basis_count):
        for s in range(species_count):
            row = radial_ref[0, b : b + 1] * lent[s : s + 1] * scale
            stacked.append(jnp.broadcast_to(row, (8, channels)))
    first = exact_dot(jnp.concatenate(stacked, axis=0), upd_ref[0])
    first_ref[...] = first
    first_t_ref[...] = first.T
    msg_t_ref[...] = msg_ref[1].T
    upd_t_ref[...] = upd_ref[1].T


def force_kernel(
    recv_ref, count_ref, hidden_ref, first_ref, first_t_ref, msg_t_ref, upd_t_ref, radial_ref, msg_ref, upd_ref, out_w_ref,
    out_ref,
    near_ref, reach_ref, inverse_ref, high_ref, low_ref, sums_ref, edge_ref, grads_ref, left_ref, slope_ref, row_h_ref,
    *, domains, slots, ghosts,
):
    groups = recv_ref.shape[0] // domains
    rows, atoms = recv_ref.shape[1:]
    reduced_dev = rows // 3
    extent = atoms + 2 * ghosts
    tail = atoms - ghosts
    species_count = count_ref.shape[0]
    basis_count, channels = radial_ref.shape[1:]
    own_chunks = atoms // LANES
    chunks = extent // LANES
    domain = lax.axis_index("space")
    scale = slots ** (-0.5)
    centers = [kappa * radial_reach * b / (basis_count - 1) for b in range(basis_count)]

    row_iota = lax.broadcasted_iota(jnp.int32, (8, atoms), 0)
    is_first = lax.rem(row_iota, 3) == 0
    segment = {}
    for step in range(-2, 3):
        shifted = domain + step + 2 * domains
        place = lax.rem(shifted, domains)
        wraps = (lax.div(shifted, domains) - 2).astype(F32) * float(domains)
        total = recv_ref[place]
        for group in range(1, groups):
            total = total + recv_ref[group * domains + place]
        if rows < 8:
            total = jnp.concatenate([total, jnp.zeros((8 - rows, atoms), F32)], axis=0)
        segment[step] = total + jnp.where(is_first, wraps, 0.0)

    def extended(step):
        return jnp.concatenate(
            [segment[step], segment[step - 1][:, tail:], segment[step + 1][:, :ghosts]], axis=1
        )

    ext_own, ext_left, ext_right = extended(0), extended(-1), extended(1)
    cols_own, cols_left, cols_right = ext_own.T, ext_left.T, ext_right.T
    lane_ext = lax.broadcasted_iota(jnp.int32, (extent, LANES), 1)
    for q in range(rows):
        near_ref[0, q] = jnp.broadcast_to(cols_own[:, q : q + 1], (extent, LANES))
        near_ref[1, q] = jnp.where(lane_ext < ghosts, cols_left[:, q : q + 1], cols_right[:, q : q + 1])

    edge_ref[...] = jnp.zeros_like(edge_ref)
    pulls = []
    for bead in range(reduced_dev):
        for chunk in range(chunks):
            lanes = slice(chunk * LANES, (chunk + 1) * LANES)
            own = chunk < own_chunks
            here = [
                jnp.broadcast_to(ext_own[bead * 3 + x : bead * 3 + x + 1, lanes], (ROWS, LANES)) for x in range(3)
            ]

            def gather_basis(step, sums, lanes=lanes, own=own, here=here):
                at = pl.ds(pl.multiple_of(step * ROWS, ROWS), ROWS)
                square = spacing_floor
                for x in range(3):
                    delta = near_ref[0 if own else 1, bead * 3 + x, at, :] - here[x]
                    square = square + delta * delta
                inverse = lax.rsqrt(square)
                reach = square * inverse * kappa
                inverse_ref[at, lanes] = inverse
                reach_ref[at, lanes] = reach
                tallies = [count_ref[s, at, lanes] for s in range(species_count)]
                if own:
                    tally = functools.reduce(jnp.add, tallies)
                sums = list(sums)
                for b in range(basis_count):
                    offset = reach - centers[b]
                    value = jnp.exp2(-(offset * offset))
                    for s in range(species_count):
                        term = tallies[s] * value
                        sums[b * species_count + s] = sums[b * species_count + s] + (term[:8] + term[8:])
                    if own:
                        high, low = halves(tally * value)
                        high_ref[b, at, lanes] = high
                        low_ref[b, at, lanes] = low
                return tuple(sums)

            zero = jnp.zeros((8, LANES), F32)
            sums = lax.fori_loop(0, extent // ROWS, gather_basis, (zero,) * (basis_count * species_count))
            for n, total in enumerate(sums):
                sums_ref[n * 8 : n * 8 + 8, lanes] = total

        update = exact_dot(first_t_ref[...], sums_ref[...])
        sigmoid = jax.nn.sigmoid(update)
        slope_ref[...] = sigmoid * (1.0 + update * (1.0 - sigmoid))
        hidden = hidden_ref[...] + update * sigmoid
        lent_t = exact_dot(msg_t_ref[...], hidden)
        lent = lent_t.T
        radial_cols = radial_ref[1].T * scale
        message = jnp.zeros((channels, atoms), F32)
        for b in range(basis_count):
            high, low = halves(lent_t * radial_cols[:, b : b + 1])
            both = fast_dot(jnp.concatenate([high, low], axis=0), high_ref[b])
            message = message + both[:channels] + both[channels:] + fast_dot(high, low_ref[b])
        update = exact_dot(upd_t_ref[...], message)
        sigmoid = jax.nn.sigmoid(update)
        out_cols = jnp.broadcast_to(out_w_ref[...], (8, channels)).T[:, 0:1]
        grad_update = out_cols * (sigmoid * (1.0 + update * (1.0 - sigmoid)))
        grad_message_t = exact_dot(upd_ref[1], grad_update)
        grad_message = grad_message_t.T

        grad_lent = jnp.zeros((extent, channels), F32)
        for b in range(basis_count):
            high, low = halves(grad_message * (radial_ref[1, b : b + 1] * scale))
            both = fast_dot(high_ref[b], jnp.concatenate([high, low], axis=1))
            grad_lent = grad_lent + both[:, :channels] + both[:, channels:] + fast_dot(low_ref[b], high)
        grad_hidden = exact_dot(msg_ref[1], grad_lent.T)
        grad_hidden = jnp.concatenate([grad_hidden[:, :atoms] + out_cols, grad_hidden[:, atoms:]], axis=1)
        row_h_ref[...] = exact_dot(first_ref[...], grad_hidden * slope_ref[...])
        high, low = halves(grad_message_t)
        grads_ref[...] = jnp.concatenate([high, high, low], axis=0)
        for b in range(basis_count):
            high, low = halves(lent * (radial_ref[1, b : b + 1] * scale))
            left_ref[b] = jnp.concatenate([high, low, high], axis=1)

        lane_row = lax.broadcasted_iota(jnp.int32, (BLOCK, LANES), 1)
        chain = -2.0 / (radial_width * math.sqrt(math.log2(math.e)))
        for own in (True, False):
            lanes = slice(0, atoms) if own else slice(atoms, extent)
            width = atoms if own else extent - atoms
            here = [ext_own[bead * 3 + x : bead * 3 + x + 1, lanes] for x in range(3)]

            def pair_grads(step, center, lanes=lanes, own=own, width=width, here=here):
                at = pl.ds(pl.multiple_of(step * BLOCK, BLOCK), BLOCK)
                reach = reach_ref[at, lanes]
                tallies = [count_ref[s, at, lanes] for s in range(species_count)]
                total = jnp.zeros((BLOCK, width), F32)
                for b in range(basis_count):
                    offset = reach - centers[b]
                    value = jnp.exp2(-(offset * offset)) * offset

                    def first_layer(s):
                        n = (b * species_count + s) * 8
                        return jnp.broadcast_to(row_h_ref[n : n + 1, lanes], (BLOCK, width))

                    slope = first_layer(0)
                    for s in range(1, species_count):
                        slope = jnp.where(tallies[s] > 0.0, first_layer(s), slope)
                    if own:
                        slope = slope + fast_dot(left_ref[b, at, :], grads_ref[...])
                    total = total + slope * value
                weight = total * functools.reduce(jnp.add, tallies) * inverse_ref[at, lanes] * chain
                center = list(center)
                columns = jnp.zeros((BLOCK, LANES), F32)
                for x in range(3):
                    near = near_ref[0 if own else 1, bead * 3 + x, at, :]
                    if width > LANES:
                        near = jnp.concatenate([near] * (width // LANES), axis=1)
                    pull = weight * (near - here[x])
                    for part in range(BLOCK // 8):
                        center[x] = center[x] + pull[part * 8 : part * 8 + 8]
                    if own:
                        columns = jnp.where(lane_row == bead * 3 + x, jnp.sum(pull, axis=1, keepdims=True), columns)
                    else:
                        left = jnp.sum(jnp.where(lane_row < ghosts, pull, 0.0), axis=1, keepdims=True)
                        right = jnp.sum(jnp.where(lane_row < ghosts, 0.0, pull), axis=1, keepdims=True)
                        columns = jnp.where(lane_row == 8 + bead * 3 + x, left, columns)
                        columns = jnp.where(lane_row == 16 + bead * 3 + x, right, columns)
                edge_ref[at, :] = edge_ref[at, :] + columns
                return tuple(center)

            zero = jnp.zeros((8, width), F32)
            center = lax.fori_loop(0, extent // BLOCK, pair_grads, (zero,) * 3)
            pulls.append([jnp.sum(c, axis=0, keepdims=True) for c in center])

    edges = edge_ref[...].T
    edge_own, edge_left, edge_right = edges[0:rows], edges[8 : 8 + rows], edges[16 : 16 + rows]
    center = jnp.concatenate(
        [
            jnp.concatenate([pulls[2 * bead][x], pulls[2 * bead + 1][x]], axis=1)
            for bead in range(reduced_dev)
            for x in range(3)
        ],
        axis=0,
    )
    edge_own = edge_own - center

    def at_head(values):
        return jnp.concatenate([values, jnp.zeros((rows, tail), F32)], axis=1)

    def at_tail(values):
        return jnp.concatenate([jnp.zeros((rows, tail), F32), values], axis=1)

    lower = slice(atoms, atoms + ghosts)
    upper = slice(atoms + ghosts, extent)
    back = {
        0: edge_own[:, :atoms] + at_head(edge_left[:, upper]) + at_tail(edge_right[:, lower]),
        -1: edge_left[:, :atoms] + at_tail(edge_own[:, lower]),
        1: edge_right[:, :atoms] + at_head(edge_own[:, upper]),
        -2: at_tail(edge_left[:, lower]),
        2: at_head(edge_right[:, upper]),
    }
    out_ref[0] = jnp.zeros_like(out_ref[0])
    for step, values in back.items():
        place = lax.rem(domain + step + 2 * domains, domains)
        out_ref[0, place] = out_ref[0, place] + values
    for group in range(1, groups):
        out_ref[group] = out_ref[0]


def on_device(
    positions, species, neighbors, counts, send_rows, embed, w_radial, w_msg, w_upd, w_out
):
    full_dev, _, atoms = positions.shape
    groups = lax.axis_size("bead")
    domains = lax.axis_size("space")
    beads_all = full_dev * groups
    reduced_dev = PC // groups
    rows = reduced_dev * 3
    slots = neighbors.shape[0]
    ghosts = send_rows.shape[0] // 2
    extent = atoms + 2 * ghosts
    species_count, channels = embed.shape
    layers, basis_count, _ = w_radial.shape
    table = jnp.asarray(contraction(beads_all, PC))
    vmem = pl.BlockSpec(memory_space=pltpu.VMEM)
    smem = pl.BlockSpec(memory_space=pltpu.SMEM)
    params = pltpu.CompilerParams(vmem_limit_bytes=VMEM_BYTES)

    def shaped(*shape):
        return jax.ShapeDtypeStruct(shape, F32)

    last = jnp.stack([species, jnp.pad(send_rows, (0, atoms - 2 * ghosts))])
    pack = jnp.concatenate([neighbors, counts[None], last], axis=0)

    def shift(values, by):
        return lax.ppermute(values, "space", [(i, (i + by) % domains) for i in range(domains)])

    from_left = shift(pack, 1)
    from_right = shift(pack, -1)
    from_far_left = shift(last, 2)
    from_far_right = from_far_left if domains == 4 else shift(last, -2)

    spread = pl.pallas_call(
        spread_kernel,
        out_shape=shaped(groups, domains, rows, atoms),
        in_specs=[smem, vmem],
        out_specs=vmem,
        compiler_params=params,
    )(table, positions)
    arrived = lax.all_to_all(
        spread.reshape(groups * domains, rows, atoms), ("bead", "space"), 0, 0, tiled=True
    )

    sums_rows = basis_count * species_count * 8
    prepared = pl.pallas_call(
        functools.partial(prepare_kernel, slots=slots, ghosts=ghosts),
        out_shape=[
            shaped(species_count, extent, extent),
            shaped(channels, extent),
            shaped(sums_rows, channels),
            shaped(channels, sums_rows),
            shaped(channels, channels),
            shaped(channels, channels),
        ],
        in_specs=[vmem] * 9,
        out_specs=[vmem] * 6,
        compiler_params=params,
    )(pack, from_left, from_right, from_far_left, from_far_right, embed, w_radial, w_msg, w_upd)

    grads = pl.pallas_call(
        functools.partial(force_kernel, domains=domains, slots=slots, ghosts=ghosts),
        out_shape=shaped(groups, domains, rows, atoms),
        in_specs=[vmem] * 11,
        out_specs=vmem,
        scratch_shapes=[
            pltpu.VMEM((2, rows, extent, LANES), F32),
            pltpu.VMEM((extent, extent), F32),
            pltpu.VMEM((extent, extent), F32),
            pltpu.VMEM((basis_count, extent, atoms), BF16),
            pltpu.VMEM((basis_count, extent, atoms), BF16),
            pltpu.VMEM((sums_rows, extent), F32),
            pltpu.VMEM((extent, LANES), F32),
            pltpu.VMEM((3 * channels, atoms), BF16),
            pltpu.VMEM((basis_count, extent, 3 * channels), BF16),
            pltpu.VMEM((channels, extent), F32),
            pltpu.VMEM((sums_rows, extent), F32),
        ],
        compiler_params=params,
    )(arrived, *prepared, w_radial, w_msg, w_upd, w_out[None])

    returned = lax.all_to_all(
        grads.reshape(groups * domains, rows, atoms), ("bead", "space"), 0, 0, tiled=True
    )
    return pl.pallas_call(
        functools.partial(collect_kernel, float(beads_all) / PC),
        out_shape=shaped(full_dev, 3, atoms),
        in_specs=[smem, vmem],
        out_specs=vmem,
        compiler_params=params,
    )(table, returned.reshape(groups, domains, rows, atoms))


def solution(mesh):
    return jax.shard_map(
        on_device,
        mesh=mesh,
        in_specs=(
            P("bead", None, "space"),
            P("space"),
            P(None, "space"),
            P("space"),
            P("space"),
            P(),
            P(),
            P(),
            P(),
            P(),
        ),
        out_specs=P("bead", None, "space"),
        check_vma=False,
    )
```

```python
import functools
import math

import jax
import jax.numpy as jnp
import numpy as np
from jax import lax
from jax.experimental import pallas as pl
from jax.experimental.pallas import tpu as pltpu
from jax.sharding import PartitionSpec as P

PC = 16

exact_mode = lax.Precision.HIGHEST
spacing_floor = 0.01
radial_width = 0.2
radial_reach = 1.5
LANES = 128
PLANES = 4
ROWS = 16
BLOCK = 64
F32 = jnp.float32
BF16 = jnp.bfloat16
UNROLL = 4
VMEM_BYTES = 48 * 1024 * 1024
kappa = math.sqrt(math.log2(math.e)) / radial_width


def contraction(full_beads, reduced_beads):
    gap = np.arange(reduced_beads)[:, None] / reduced_beads - np.arange(full_beads)[None, :] / full_beads
    total = np.ones_like(gap)
    for harmonic in range(1, reduced_beads // 2):
        total = total + 2.0 * np.cos(2.0 * np.pi * harmonic * gap)
    total = total + np.cos(np.pi * reduced_beads * gap)
    return (total / full_beads).astype(np.float32)


def exact_dot(left, right):
    return lax.dot(left, right, precision=exact_mode, preferred_element_type=F32)


def near_dot(left, right):
    return lax.dot(left, right, precision=lax.Precision.HIGH, preferred_element_type=F32)


def fast_dot(left, right):
    return lax.dot(left, right, preferred_element_type=F32)


def halves(values):
    high = values.astype(BF16)
    low = (values - high.astype(F32)).astype(BF16)
    return high, low


def spread_kernel(table_ref, pos_ref, out_ref):
    components, full_dev, atoms = pos_ref.shape
    groups, domains, rows, _ = out_ref.shape
    values = pos_ref[...].reshape(components * full_dev, atoms)
    total = exact_dot(table_ref[lax.axis_index("bead")], values).reshape(groups, rows, atoms)
    for domain in range(domains):
        out_ref[:, domain] = total


def collect_kernel(table_ref, in_ref, out_ref):
    groups, domains, rows, atoms = in_ref.shape
    total = in_ref[:, 0]
    for domain in range(1, domains):
        total = total + in_ref[:, domain]
    out = exact_dot(table_ref[lax.axis_index("bead")], total.reshape(groups * rows, atoms))
    out_ref[...] = out.reshape(out_ref.shape)


def spread_tables(beads_all, groups, pad_rows):
    table = contraction(beads_all, PC)
    full_dev, reduced_dev = beads_all // groups, PC // groups
    out = np.zeros((groups, groups, pad_rows, 3, full_dev), np.float32)
    for own in range(groups):
        for group in range(groups):
            part = table[group * reduced_dev : (group + 1) * reduced_dev, own * full_dev : (own + 1) * full_dev]
            for x in range(3):
                out[own, group, x * reduced_dev : (x + 1) * reduced_dev, x] = part
    out = out.reshape(groups, groups * pad_rows, 3 * full_dev)
    back = -(beads_all / PC) * out.transpose(0, 2, 1)
    return jnp.asarray(out), jnp.asarray(np.ascontiguousarray(back.astype(np.float32)))


def prepare_kernel(
    own_ref, left_ref, right_ref, far_left_ref, far_right_ref, embed_ref, radial_ref, msg_ref, upd_ref,
    count_ref, hidden_ref, first_ref, first_t_ref, msg_t_ref, upd_t_ref, fan_ref, fold_ref,
    *, slots, ghosts,
):
    atoms = own_ref.shape[1]
    extent = atoms + 2 * ghosts
    species_count, channels = embed_ref.shape
    basis_count = radial_ref.shape[1]
    tail = atoms - ghosts
    count_row, species_row, send_row = slots, slots + 1, slots + 2

    def edge_pack(row, rows=1):
        return jnp.concatenate(
            [own_ref[row : row + rows], left_ref[row : row + rows, tail:], right_ref[row : row + rows, :ghosts]],
            axis=1,
        )

    neighbors = edge_pack(0, slots)
    counts = edge_pack(count_row)
    own_send = own_ref[send_row : send_row + 1]
    left_send = left_ref[send_row : send_row + 1]
    right_send = right_ref[send_row : send_row + 1]
    far_left_send = far_left_ref[1:2]
    far_right_send = far_right_ref[1:2]

    def ghost_map(from_left, from_right):
        return jnp.concatenate(
            [from_left[:, ghosts : 2 * ghosts] - tail, from_right[:, :ghosts] + ghosts], axis=1
        )

    maps = [
        ghost_map(left_send, right_send),
        ghost_map(far_left_send, own_send),
        ghost_map(own_send, far_right_send),
    ]
    maps = [jnp.broadcast_to(m, (slots, 2 * ghosts)) for m in maps]
    lane = lax.broadcasted_iota(jnp.int32, (slots, LANES), 1)
    slot = lax.broadcasted_iota(jnp.int32, (slots, LANES), 0)

    species_rows = []
    for near, lower, upper in (
        (own_ref[species_row : species_row + 1], left_ref[species_row : species_row + 1], right_ref[species_row : species_row + 1]),
        (left_ref[species_row : species_row + 1], far_left_ref[0:1], own_ref[species_row : species_row + 1]),
        (right_ref[species_row : species_row + 1], own_ref[species_row : species_row + 1], far_right_ref[0:1]),
    ):
        species_rows.append(jnp.concatenate([near, lower[:, tail:], upper[:, :ghosts]], axis=1))
    species_f = jnp.concatenate(species_rows + [species_rows[0]] * 5, axis=0).astype(F32)
    species_cols = species_f.T

    plane_rows = extent // PLANES
    chunks = extent // LANES
    plane_iota = lax.broadcasted_iota(jnp.int32, (plane_rows, LANES), 0)
    lane_block = lax.broadcasted_iota(jnp.int32, (plane_rows, LANES), 1)
    for chunk in range(chunks):
        lanes = slice(chunk * LANES, (chunk + 1) * LANES)
        rows_now = neighbors[:, lanes]
        index = jnp.clip(rows_now - atoms, 0, 2 * ghosts - 1)
        if (chunk + 1) * LANES <= atoms:
            mapped = jnp.take_along_axis(maps[0], index, axis=1, mode="promise_in_bounds")
        else:
            mapped = jnp.where(
                lane < ghosts,
                jnp.take_along_axis(maps[1], index, axis=1, mode="promise_in_bounds"),
                jnp.take_along_axis(maps[2], index, axis=1, mode="promise_in_bounds"),
            )
        rows_now = jnp.where(rows_now >= atoms, atoms + mapped, rows_now)
        plane = jnp.zeros_like(rows_now)
        for step in range(1, PLANES):
            plane = plane + (rows_now >= step * plane_rows).astype(jnp.int32)
        within = rows_now - plane * plane_rows
        within = jnp.where(slot < counts[:, lanes], within, -1)
        value = jnp.left_shift(jnp.ones_like(plane), 8 * plane)
        words = jnp.zeros((plane_rows, LANES), jnp.int32)
        for k in range(slots):
            words = words + jnp.where(within[k : k + 1] == plane_iota, value[k : k + 1], 0)
        for step in range(PLANES):
            rows = slice(step * plane_rows, (step + 1) * plane_rows)
            tally = (jnp.right_shift(words, 8 * step) & 255).astype(F32)
            if (chunk + 1) * LANES <= atoms:
                kind = jnp.broadcast_to(species_cols[rows, 0:1], (plane_rows, LANES))
            else:
                kind = jnp.where(lane_block < ghosts, species_cols[rows, 1:2], species_cols[rows, 2:3])
            for s in range(species_count):
                count_ref[s, rows, lanes] = jnp.where(kind == float(s), tally, 0.0)

    embed = embed_ref[...]
    embed_pad = jnp.concatenate([embed, jnp.zeros((8 - species_count, channels), F32)], axis=0)
    embed_cols = embed_pad.T
    hidden = jnp.zeros((channels, extent), F32)
    for s in range(species_count):
        hidden = hidden + embed_cols[:, s : s + 1] * (species_f[0:1] == float(s)).astype(F32)
    hidden_ref[...] = hidden

    scale = slots ** (-0.5)
    lent = exact_dot(embed_pad, msg_ref[0])
    stacked = []
    for b in range(basis_count):
        for s in range(species_count):
            row = radial_ref[0, b : b + 1] * lent[s : s + 1] * scale
            stacked.append(jnp.broadcast_to(row, (8, channels)))
    first = exact_dot(jnp.concatenate(stacked, axis=0), upd_ref[0])
    first_ref[...] = first
    first_t_ref[...] = first.T
    msg_t_ref[...] = msg_ref[1].T
    upd_t_ref[...] = upd_ref[1].T

    row = lax.broadcasted_iota(jnp.int32, fan_ref.shape, 0)
    column = lax.broadcasted_iota(jnp.int32, fan_ref.shape, 1)
    part = lax.rem(column, 2 * LANES)
    part = (part >= LANES).astype(jnp.int32) + (part >= LANES + ghosts).astype(jnp.int32)
    pad_rows = fan_ref.shape[0] // 9
    fan_ref[...] = jnp.where(
        lax.rem(row, 3 * pad_rows) == part * pad_rows + lax.div(column, 2 * LANES), 1.0, 0.0
    ).astype(BF16)
    row = lax.broadcasted_iota(jnp.int32, fold_ref.shape, 0)
    column = lax.broadcasted_iota(jnp.int32, fold_ref.shape, 1)
    part = jnp.where(
        lax.rem(row, 4 * LANES) < 2 * LANES, 0, jnp.where(lax.rem(row, LANES) < ghosts, 1, 2)
    )
    fold_ref[...] = jnp.where(column == part * pad_rows + lax.div(row, 4 * LANES), 1.0, 0.0).astype(BF16)


def force_kernel(
    recv_ref, count_ref, hidden_ref, first_ref, first_t_ref, msg_t_ref, upd_t_ref, fan_ref, fold_ref, radial_ref, msg_ref, upd_ref, out_w_ref,
    out_ref,
    near_ref, reach_ref, inverse_ref, high_ref, low_ref, sums_ref, edge_ref, slope_pair_ref, slope_ref, row_h_ref, wide_ref,
    *, domains, slots, ghosts, reduced_dev,
):
    groups = recv_ref.shape[0] // domains
    pad_rows, atoms = recv_ref.shape[1:]
    rows = reduced_dev * 3
    extent = atoms + 2 * ghosts
    tail = atoms - ghosts
    species_count = count_ref.shape[0]
    basis_count, channels = radial_ref.shape[1:]
    own_chunks = atoms // LANES
    chunks = extent // LANES
    beads = range(reduced_dev)
    domain = lax.axis_index("space")
    scale = slots ** (-0.5)
    centers = [kappa * radial_reach * b / (basis_count - 1) for b in range(basis_count)]

    is_first = lax.broadcasted_iota(jnp.int32, (pad_rows, atoms), 0) < reduced_dev
    segment = {}
    for step in range(-2, 3):
        shifted = domain + step + 2 * domains
        place = lax.rem(shifted, domains)
        wraps = (lax.div(shifted, domains) - 2).astype(F32) * float(domains)
        total = recv_ref[place]
        for group in range(1, groups):
            total = total + recv_ref[group * domains + place]
        segment[step] = total + jnp.where(is_first, wraps, 0.0)

    def extended(step):
        return jnp.concatenate(
            [segment[step], segment[step - 1][:, tail:], segment[step + 1][:, :ghosts]], axis=1
        )

    ext_own, ext_left, ext_right = extended(0), extended(-1), extended(1)
    stacked = jnp.concatenate([ext_own, ext_left, ext_right], axis=0)
    high = stacked.astype(BF16).astype(F32)
    middle = (stacked - high).astype(BF16).astype(F32)
    parts = jnp.concatenate([high, middle, stacked - high - middle], axis=0)
    near_ref[...] = fast_dot(parts.T.astype(BF16), fan_ref[...])

    def near(own, q, at):
        start = (2 * q + (0 if own else 1)) * LANES
        return near_ref[at, start : start + LANES]


    for bead in beads:
        for chunk in range(chunks):
            lanes = slice(chunk * LANES, (chunk + 1) * LANES)
            own = chunk < own_chunks
            here = [
                jnp.broadcast_to(ext_own[x * reduced_dev + bead : x * reduced_dev + bead + 1, lanes], (ROWS, LANES))
                for x in range(3)
            ]

            def gather_basis(step, sums, bead=bead, lanes=lanes, own=own, here=here):
                at = pl.ds(pl.multiple_of(step * ROWS, ROWS), ROWS)
                square = spacing_floor
                for x in range(3):
                    delta = near(own, x * reduced_dev + bead, at) - here[x]
                    square = square + delta * delta
                inverse = lax.rsqrt(square)
                reach = square * inverse * kappa
                inverse_ref[bead, at, lanes] = inverse
                reach_ref[bead, at, lanes] = reach
                tallies = [count_ref[s, at, lanes] for s in range(species_count)]
                tally = functools.reduce(jnp.add, tallies)
                sums = list(sums)
                for b in range(basis_count):
                    offset = reach - centers[b]
                    value = jnp.exp2(-(offset * offset))
                    for s in range(species_count):
                        term = tallies[s] * value
                        sums[b * species_count + s] = sums[b * species_count + s] + (term[:8] + term[8:])
                    if own:
                        high, low = halves(tally * value)
                        high_ref[bead, b, at, lanes] = high
                        low_ref[bead, b, at, lanes] = low
                return tuple(sums)

            zero = jnp.zeros((8, LANES), F32)
            sums = lax.fori_loop(0, extent // ROWS, gather_basis, (zero,) * (basis_count * species_count), unroll=UNROLL)
            for n, total in enumerate(sums):
                start = bead * extent + chunk * LANES
                sums_ref[n * 8 : n * 8 + 8, start : start + LANES] = total

    update = near_dot(first_t_ref[...], sums_ref[...])
    sigmoid = jax.nn.sigmoid(update)
    slope_ref[...] = sigmoid * (1.0 + update * (1.0 - sigmoid))
    hidden = jnp.concatenate([hidden_ref[...]] * reduced_dev, axis=1) + update * sigmoid
    lent_t = near_dot(msg_t_ref[...], hidden)
    lent = lent_t.T
    radial_cols = radial_ref[1].T * scale
    messages = []
    for bead in beads:
        for b in range(basis_count):
            high, low = halves(lent_t[:, bead * extent : (bead + 1) * extent] * radial_cols[:, b : b + 1])
            wide_ref[:channels, b * extent : (b + 1) * extent] = high
            wide_ref[channels:, b * extent : (b + 1) * extent] = low
        both = fast_dot(wide_ref[...], high_ref[bead].reshape(basis_count * extent, atoms))
        last = fast_dot(wide_ref[:channels], low_ref[bead].reshape(basis_count * extent, atoms))
        messages.append(both[:channels] + both[channels:] + last)
    message = jnp.concatenate(messages, axis=1)
    update = near_dot(upd_t_ref[...], message)
    sigmoid = jax.nn.sigmoid(update)
    out_cols = jnp.broadcast_to(out_w_ref[...], (8, channels)).T[:, 0:1]
    grad_update = out_cols * (sigmoid * (1.0 + update * (1.0 - sigmoid)))
    grad_message_t = near_dot(upd_ref[1], grad_update)
    grad_message = grad_message_t.T

    grads_lent = []
    for bead in beads:
        grad_lent = jnp.zeros((extent, channels), F32)
        for b in range(basis_count):
            high, low = halves(grad_message[bead * atoms : (bead + 1) * atoms] * (radial_ref[1, b : b + 1] * scale))
            both = fast_dot(high_ref[bead, b], jnp.concatenate([high, low], axis=1))
            grad_lent = grad_lent + both[:, :channels] + both[:, channels:] + fast_dot(low_ref[bead, b], high)
        grads_lent.append(grad_lent)
    grad_hidden = near_dot(msg_ref[1], jnp.concatenate(grads_lent, axis=0).T)
    parts = []
    for bead in beads:
        start = bead * extent
        parts += [grad_hidden[:, start : start + atoms] + out_cols, grad_hidden[:, start + atoms : start + extent]]
    row_h_ref[...] = near_dot(first_ref[...], jnp.concatenate(parts, axis=1) * slope_ref[...])
    for bead in beads:
        high, low = halves(grad_message_t[:, bead * atoms : (bead + 1) * atoms])
        grads = jnp.concatenate([high, high, low], axis=0)
        for b in range(basis_count):
            high, low = halves(lent[bead * extent : (bead + 1) * extent] * (radial_ref[1, b : b + 1] * scale))
            slope_pair_ref[bead, b] = fast_dot(jnp.concatenate([high, low, high], axis=1), grads)

    pulls = []
    chain = -2.0 / (radial_width * math.sqrt(math.log2(math.e)))
    for bead in beads:
        for own in (True, False):
            lanes = slice(0, atoms) if own else slice(atoms, extent)
            width = atoms if own else extent - atoms
            start = bead * extent + lanes.start
            here = [ext_own[x * reduced_dev + bead : x * reduced_dev + bead + 1, lanes] for x in range(3)]

            def pair_grads(step, center, bead=bead, lanes=lanes, own=own, width=width, here=here, start=start):
                at = pl.ds(pl.multiple_of(step * BLOCK, BLOCK), BLOCK)
                reach = reach_ref[bead, at, lanes]
                tallies = [count_ref[s, at, lanes] for s in range(species_count)]
                total = jnp.zeros((BLOCK, width), F32)
                for b in range(basis_count):
                    offset = reach - centers[b]
                    value = jnp.exp2(-(offset * offset)) * offset

                    def first_layer(s):
                        n = (b * species_count + s) * 8
                        tile = row_h_ref[n : n + 8, start : start + width]
                        return jnp.concatenate([tile] * (BLOCK // 8), axis=0)

                    slope = first_layer(0)
                    for s in range(1, species_count):
                        slope = jnp.where(tallies[s] > 0.0, first_layer(s), slope)
                    if own:
                        slope = slope + slope_pair_ref[bead, b, at, :]
                    total = total + slope * value
                weight = total * functools.reduce(jnp.add, tallies) * inverse_ref[bead, at, lanes] * chain
                center = list(center)
                for x in range(3):
                    q = x * reduced_dev + bead
                    place = near(own, q, at)
                    folded = None
                    for chunk in range(width // LANES):
                        cut = slice(chunk * LANES, (chunk + 1) * LANES)
                        pull = weight[:, cut] * (place - here[x][:, cut])
                        folded = pull if folded is None else folded + pull
                        n = x * (width // LANES) + chunk
                        for part in range(BLOCK // 8):
                            center[n] = center[n] + pull[part * 8 : part * 8 + 8]
                    high, low = halves(folded)
                    start_q = (2 * q + (0 if own else 1)) * 2 * LANES
                    edge_ref[at, start_q : start_q + LANES] = high
                    edge_ref[at, start_q + LANES : start_q + 2 * LANES] = low
                return tuple(center)

            zero = jnp.zeros((8, LANES), F32)
            many = width // LANES
            center = lax.fori_loop(0, extent // BLOCK, pair_grads, (zero,) * (3 * many))
            pulls.append(
                [
                    jnp.concatenate(
                        [jnp.sum(c, axis=0, keepdims=True) for c in center[x * many : (x + 1) * many]], axis=1
                    )
                    for x in range(3)
                ]
            )

    edges = fast_dot(edge_ref[...], fold_ref[...]).T
    edge_own, edge_left, edge_right = (edges[pad_rows * n : pad_rows * (n + 1)] for n in range(3))
    center = [
        jnp.concatenate([pulls[2 * bead][x], pulls[2 * bead + 1][x]], axis=1) for x in range(3) for bead in beads
    ]
    if rows < pad_rows:
        center.append(jnp.zeros((pad_rows - rows, extent), F32))
    edge_own = edge_own - jnp.concatenate(center, axis=0)

    def at_head(values):
        return jnp.concatenate([values, jnp.zeros((pad_rows, tail), F32)], axis=1)

    def at_tail(values):
        return jnp.concatenate([jnp.zeros((pad_rows, tail), F32), values], axis=1)

    lower = slice(atoms, atoms + ghosts)
    upper = slice(atoms + ghosts, extent)
    back = {
        0: edge_own[:, :atoms] + at_head(edge_left[:, upper]) + at_tail(edge_right[:, lower]),
        -1: edge_left[:, :atoms] + at_tail(edge_own[:, lower]),
        1: edge_right[:, :atoms] + at_head(edge_own[:, upper]),
        -2: at_tail(edge_left[:, lower]),
        2: at_head(edge_right[:, upper]),
    }
    out_ref[0] = jnp.zeros_like(out_ref[0])
    for step, values in back.items():
        place = lax.rem(domain + step + 2 * domains, domains)
        out_ref[0, place] = out_ref[0, place] + values
    for group in range(1, groups):
        out_ref[group] = out_ref[0]


def on_device(
    positions, species, neighbors, counts, send_rows, embed, w_radial, w_msg, w_upd, w_out
):
    full_dev, _, atoms = positions.shape
    groups = lax.axis_size("bead")
    domains = lax.axis_size("space")
    beads_all = full_dev * groups
    reduced_dev = PC // groups
    rows = -(-reduced_dev * 3 // 8) * 8
    slots = neighbors.shape[0]
    ghosts = send_rows.shape[0] // 2
    extent = atoms + 2 * ghosts
    species_count, channels = embed.shape
    layers, basis_count, _ = w_radial.shape
    table, back_table = spread_tables(beads_all, groups, rows)
    vmem = pl.BlockSpec(memory_space=pltpu.VMEM)
    params = pltpu.CompilerParams(vmem_limit_bytes=VMEM_BYTES)

    def shaped(*shape):
        return jax.ShapeDtypeStruct(shape, F32)

    last = jnp.stack([species, jnp.pad(send_rows, (0, atoms - 2 * ghosts))])
    pack = jnp.concatenate([neighbors, counts[None], last], axis=0)

    def shift(values, by):
        return lax.ppermute(values, "space", [(i, (i + by) % domains) for i in range(domains)])

    from_left = shift(pack, 1)
    from_right = shift(pack, -1)
    from_far_left = shift(last, 2)
    from_far_right = from_far_left if domains == 4 else shift(last, -2)

    spread = pl.pallas_call(
        spread_kernel,
        out_shape=shaped(groups, domains, rows, atoms),
        in_specs=[vmem, vmem],
        out_specs=vmem,
        compiler_params=params,
    )(table, positions.transpose(1, 0, 2))
    arrived = lax.all_to_all(
        spread.reshape(groups * domains, rows, atoms), ("bead", "space"), 0, 0, tiled=True
    )

    sums_rows = basis_count * species_count * 8
    lane_count = 2 * LANES * 3 * reduced_dev
    prepared = pl.pallas_call(
        functools.partial(prepare_kernel, slots=slots, ghosts=ghosts),
        out_shape=[
            shaped(species_count, extent, extent),
            shaped(channels, extent),
            shaped(sums_rows, channels),
            shaped(channels, sums_rows),
            shaped(channels, channels),
            shaped(channels, channels),
            jax.ShapeDtypeStruct((9 * rows, lane_count), BF16),
            jax.ShapeDtypeStruct((2 * lane_count, LANES), BF16),
        ],
        in_specs=[vmem] * 9,
        out_specs=[vmem] * 8,
        compiler_params=params,
    )(pack, from_left, from_right, from_far_left, from_far_right, embed, w_radial, w_msg, w_upd)

    grads = pl.pallas_call(
        functools.partial(force_kernel, domains=domains, slots=slots, ghosts=ghosts, reduced_dev=reduced_dev),
        out_shape=shaped(groups, domains, rows, atoms),
        in_specs=[vmem] * 13,
        out_specs=vmem,
        scratch_shapes=[
            pltpu.VMEM((extent, lane_count), F32),
            pltpu.VMEM((reduced_dev, extent, extent), F32),
            pltpu.VMEM((reduced_dev, extent, extent), F32),
            pltpu.VMEM((reduced_dev, basis_count, extent, atoms), BF16),
            pltpu.VMEM((reduced_dev, basis_count, extent, atoms), BF16),
            pltpu.VMEM((sums_rows, reduced_dev * extent), F32),
            pltpu.VMEM((extent, 2 * lane_count), BF16),
            pltpu.VMEM((reduced_dev, basis_count, extent, atoms), F32),
            pltpu.VMEM((channels, reduced_dev * extent), F32),
            pltpu.VMEM((sums_rows, reduced_dev * extent), F32),
            pltpu.VMEM((2 * channels, basis_count * extent), BF16),
        ],
        compiler_params=params,
    )(arrived, *prepared, w_radial, w_msg, w_upd, w_out[None])

    returned = lax.all_to_all(
        grads.reshape(groups * domains, rows, atoms), ("bead", "space"), 0, 0, tiled=True
    )
    forces = pl.pallas_call(
        collect_kernel,
        out_shape=shaped(3, full_dev, atoms),
        in_specs=[vmem, vmem],
        out_specs=vmem,
        compiler_params=params,
    )(back_table, returned.reshape(groups, domains, rows, atoms))
    return forces.transpose(1, 0, 2)


def solution(mesh):
    return jax.shard_map(
        on_device,
        mesh=mesh,
        in_specs=(
            P("bead", None, "space"),
            P("space"),
            P(None, "space"),
            P("space"),
            P("space"),
            P(),
            P(),
            P(),
            P(),
            P(),
        ),
        out_specs=P("bead", None, "space"),
        check_vma=False,
    )
```

```python
import functools
import math

import jax
import jax.numpy as jnp
import numpy as np
from jax import lax
from jax.experimental import pallas as pl
from jax.experimental.pallas import tpu as pltpu
from jax.sharding import PartitionSpec as P

PC = 16

exact_mode = lax.Precision.HIGHEST
spacing_floor = 0.01
radial_width = 0.2
radial_reach = 1.5
LANES = 128
PLANES = 4
ROWS = 16
BLOCK = 64
F32 = jnp.float32
BF16 = jnp.bfloat16
UNROLL = 24
VMEM_BYTES = 48 * 1024 * 1024
kappa = math.sqrt(math.log2(math.e)) / radial_width


def contraction(full_beads, reduced_beads):
    gap = np.arange(reduced_beads)[:, None] / reduced_beads - np.arange(full_beads)[None, :] / full_beads
    total = np.ones_like(gap)
    for harmonic in range(1, reduced_beads // 2):
        total = total + 2.0 * np.cos(2.0 * np.pi * harmonic * gap)
    total = total + np.cos(np.pi * reduced_beads * gap)
    return (total / full_beads).astype(np.float32)


def exact_dot(left, right):
    return lax.dot(left, right, precision=exact_mode, preferred_element_type=F32)


def near_dot(left, right):
    return lax.dot(left, right, precision=lax.Precision.HIGH, preferred_element_type=F32)


def fast_dot(left, right):
    return lax.dot(left, right, preferred_element_type=F32)


def halves(values):
    high = values.astype(BF16)
    low = (values - high.astype(F32)).astype(BF16)
    return high, low


def spread_kernel(pos_ref, out_ref):
    components, full_dev, atoms = pos_ref.shape
    groups, domains, rows, _ = out_ref.shape
    reduced_dev = PC // groups
    beads_all = groups * full_dev
    k = lax.broadcasted_iota(jnp.int32, (PC, full_dev), 0).astype(F32)
    j = lax.broadcasted_iota(jnp.int32, (PC, full_dev), 1) + lax.axis_index("bead") * full_dev
    gap = k / PC - j.astype(F32) / beads_all
    table = jnp.ones_like(gap)
    for harmonic in range(1, PC // 2 + 1):
        turn = gap * harmonic
        wave = jnp.cos((turn - jnp.floor(turn)) * (2.0 * math.pi))
        table = table + (wave if harmonic == PC // 2 else 2.0 * wave)
    table = table / beads_all
    total = exact_dot(table, jnp.concatenate([pos_ref[x] for x in range(components)], axis=1))
    for group in range(groups):
        at = slice(group * reduced_dev, (group + 1) * reduced_dev)
        parts = [total[at, x * atoms : (x + 1) * atoms] for x in range(components)]
        if rows > 3 * reduced_dev:
            parts.append(jnp.zeros((rows - 3 * reduced_dev, atoms), F32))
        block = jnp.concatenate(parts, axis=0)
        for domain in range(domains):
            out_ref[group, domain] = block


def collect_kernel(table_ref, in_ref, out_ref):
    groups, domains, rows, atoms = in_ref.shape
    total = in_ref[:, 0]
    for domain in range(1, domains):
        total = total + in_ref[:, domain]
    out = exact_dot(table_ref[lax.axis_index("bead")], total.reshape(groups * rows, atoms))
    out_ref[...] = out.reshape(out_ref.shape)


def collect_table(beads_all, groups, pad_rows):
    table = contraction(beads_all, PC)
    full_dev, reduced_dev = beads_all // groups, PC // groups
    out = np.zeros((groups, 3, full_dev, groups, pad_rows), np.float32)
    for own in range(groups):
        for group in range(groups):
            part = table[group * reduced_dev : (group + 1) * reduced_dev, own * full_dev : (own + 1) * full_dev]
            for x in range(3):
                out[own, x, :, group, x * reduced_dev : (x + 1) * reduced_dev] = part.T
    return jnp.asarray(-(beads_all / PC) * out.reshape(groups, 3 * full_dev, groups * pad_rows))


def weights_kernel(
    embed_ref, radial_ref, msg_ref, upd_ref,
    embed_cols_ref, first_ref, first_t_ref, msg_t_ref, upd_t_ref, fan_ref,
    *, slots, ghosts,
):
    species_count, channels = embed_ref.shape
    basis_count = radial_ref.shape[1]
    embed = embed_ref[...]
    embed_pad = jnp.concatenate([embed, jnp.zeros((8 - species_count, channels), F32)], axis=0)
    embed_cols_ref[...] = embed_pad.T
    scale = slots ** (-0.5)
    lent = exact_dot(embed_pad, msg_ref[0])
    stacked = []
    for b in range(basis_count):
        for s in range(species_count):
            row = radial_ref[0, b : b + 1] * lent[s : s + 1] * scale
            stacked.append(jnp.broadcast_to(row, (8, channels)))
    first = exact_dot(jnp.concatenate(stacked, axis=0), upd_ref[0])
    first_ref[...] = first
    first_t_ref[...] = first.T
    msg_t_ref[...] = msg_ref[1].T
    upd_t_ref[...] = upd_ref[1].T

    row = lax.broadcasted_iota(jnp.int32, fan_ref.shape, 0)
    column = lax.broadcasted_iota(jnp.int32, fan_ref.shape, 1)
    part = lax.rem(column, 2 * LANES)
    part = (part >= LANES).astype(jnp.int32) + (part >= LANES + ghosts).astype(jnp.int32)
    pad_rows = fan_ref.shape[0] // 9
    fan_ref[...] = jnp.where(
        lax.rem(row, 3 * pad_rows) == part * pad_rows + lax.div(column, 2 * LANES), 1.0, 0.0
    ).astype(BF16)


def counts_kernel(
    own_ref, left_ref, right_ref, far_left_ref, far_right_ref, embed_cols_ref, count_ref, hidden_ref, *, slots, ghosts
):
    atoms = own_ref.shape[1]
    channels = embed_cols_ref.shape[0]
    species_count = count_ref.shape[0]
    extent = atoms + 2 * ghosts
    tail = atoms - ghosts
    count_row, species_row, send_row = slots, slots + 1, slots + 2

    def edge_pack(row, rows=1):
        return jnp.concatenate(
            [own_ref[row : row + rows], left_ref[row : row + rows, tail:], right_ref[row : row + rows, :ghosts]],
            axis=1,
        )

    neighbors = edge_pack(0, slots)
    counts = edge_pack(count_row)
    own_send = own_ref[send_row : send_row + 1]
    left_send = left_ref[send_row : send_row + 1]
    right_send = right_ref[send_row : send_row + 1]
    far_left_send = far_left_ref[send_row : send_row + 1]
    far_right_send = far_right_ref[send_row : send_row + 1]

    def ghost_map(from_left, from_right):
        return jnp.concatenate(
            [from_left[:, ghosts : 2 * ghosts] - tail, from_right[:, :ghosts] + ghosts], axis=1
        )

    maps = [
        ghost_map(left_send, right_send),
        ghost_map(far_left_send, own_send),
        ghost_map(own_send, far_right_send),
    ]
    maps = [jnp.broadcast_to(m, (slots, 2 * ghosts)) for m in maps]
    lane = lax.broadcasted_iota(jnp.int32, (slots, LANES), 1)
    slot = lax.broadcasted_iota(jnp.int32, (slots, LANES), 0)

    species_rows = []
    for near, lower, upper in (
        (own_ref[species_row : species_row + 1], left_ref[species_row : species_row + 1], right_ref[species_row : species_row + 1]),
        (left_ref[species_row : species_row + 1], far_left_ref[species_row : species_row + 1], own_ref[species_row : species_row + 1]),
        (right_ref[species_row : species_row + 1], own_ref[species_row : species_row + 1], far_right_ref[species_row : species_row + 1]),
    ):
        species_rows.append(jnp.concatenate([near, lower[:, tail:], upper[:, :ghosts]], axis=1))
    species_f = jnp.concatenate(species_rows + [species_rows[0]] * 5, axis=0).astype(F32)
    species_cols = species_f.T

    plane_rows = extent // PLANES
    chunks = extent // LANES
    plane_iota = lax.broadcasted_iota(jnp.int32, (plane_rows, LANES), 0)
    lane_block = lax.broadcasted_iota(jnp.int32, (plane_rows, LANES), 1)
    for chunk in range(chunks):
        lanes = slice(chunk * LANES, (chunk + 1) * LANES)
        rows_now = neighbors[:, lanes]
        index = jnp.clip(rows_now - atoms, 0, 2 * ghosts - 1)
        if (chunk + 1) * LANES <= atoms:
            mapped = jnp.take_along_axis(maps[0], index, axis=1, mode="promise_in_bounds")
        else:
            mapped = jnp.where(
                lane < ghosts,
                jnp.take_along_axis(maps[1], index, axis=1, mode="promise_in_bounds"),
                jnp.take_along_axis(maps[2], index, axis=1, mode="promise_in_bounds"),
            )
        rows_now = jnp.where(rows_now >= atoms, atoms + mapped, rows_now)
        plane = jnp.zeros_like(rows_now)
        for step in range(1, PLANES):
            plane = plane + (rows_now >= step * plane_rows).astype(jnp.int32)
        within = rows_now - plane * plane_rows
        within = jnp.where(slot < counts[:, lanes], within, -1)
        value = jnp.left_shift(jnp.ones_like(plane), 8 * plane)
        words = jnp.zeros((plane_rows, LANES), jnp.int32)
        for k in range(slots):
            words = words + jnp.where(within[k : k + 1] == plane_iota, value[k : k + 1], 0)
        for step in range(PLANES):
            rows = slice(step * plane_rows, (step + 1) * plane_rows)
            tally = (jnp.right_shift(words, 8 * step) & 255).astype(F32)
            if (chunk + 1) * LANES <= atoms:
                kind = jnp.broadcast_to(species_cols[rows, 0:1], (plane_rows, LANES))
            else:
                kind = jnp.where(lane_block < ghosts, species_cols[rows, 1:2], species_cols[rows, 2:3])
            for s in range(species_count):
                count_ref[s, rows, lanes] = jnp.where(kind == float(s), tally, 0.0)

    hidden = jnp.zeros((channels, extent), F32)
    for s in range(species_count):
        hidden = hidden + embed_cols_ref[:, s : s + 1] * (species_f[0:1] == float(s)).astype(F32)
    hidden_ref[...] = hidden


def force_kernel(
    recv_ref, count_ref, hidden_ref, first_ref, first_t_ref, msg_t_ref, upd_t_ref, fan_ref, radial_ref, msg_ref, upd_ref, out_w_ref,
    out_ref,
    near_ref, inverse_ref, high_ref, low_ref, sums_ref, edge_ref, slope_pair_ref, slope_ref, row_h_ref, wide_ref, wave_ref,
    *, domains, slots, ghosts, reduced_dev,
):
    groups = recv_ref.shape[0] // domains
    pad_rows, atoms = recv_ref.shape[1:]
    rows = reduced_dev * 3
    extent = atoms + 2 * ghosts
    tail = atoms - ghosts
    species_count = count_ref.shape[0]
    basis_count, channels = radial_ref.shape[1:]
    own_chunks = atoms // LANES
    chunks = extent // LANES
    beads = range(reduced_dev)
    domain = lax.axis_index("space")
    scale = slots ** (-0.5)
    centers = [kappa * radial_reach * b / (basis_count - 1) for b in range(basis_count)]

    is_first = lax.broadcasted_iota(jnp.int32, (pad_rows, atoms), 0) < reduced_dev
    segment = {}
    for step in range(-2, 3):
        shifted = domain + step + 2 * domains
        place = lax.rem(shifted, domains)
        wraps = (lax.div(shifted, domains) - 2).astype(F32) * float(domains)
        total = recv_ref[place]
        for group in range(1, groups):
            total = total + recv_ref[group * domains + place]
        segment[step] = total + jnp.where(is_first, wraps, 0.0)

    def extended(step):
        return jnp.concatenate(
            [segment[step], segment[step - 1][:, tail:], segment[step + 1][:, :ghosts]], axis=1
        )

    ext_own, ext_left, ext_right = extended(0), extended(-1), extended(1)
    stacked = jnp.concatenate([ext_own, ext_left, ext_right], axis=0)
    high = stacked.astype(BF16).astype(F32)
    middle = (stacked - high).astype(BF16).astype(F32)
    parts = jnp.concatenate([high, middle, stacked - high - middle], axis=0)
    near_ref[...] = fast_dot(parts.T.astype(BF16), fan_ref[...])

    def near(own, q, at):
        start = (2 * q + (0 if own else 1)) * LANES
        return near_ref[at, start : start + LANES]


    for bead in beads:
        for chunk in range(chunks):
            lanes = slice(chunk * LANES, (chunk + 1) * LANES)
            own = chunk < own_chunks
            here = [
                jnp.broadcast_to(ext_own[x * reduced_dev + bead : x * reduced_dev + bead + 1, lanes], (ROWS, LANES))
                for x in range(3)
            ]

            def gather_basis(step, sums, bead=bead, lanes=lanes, own=own, here=here):
                at = pl.ds(pl.multiple_of(step * ROWS, ROWS), ROWS)
                square = spacing_floor
                for x in range(3):
                    delta = near(own, x * reduced_dev + bead, at) - here[x]
                    square = square + delta * delta
                inverse = lax.rsqrt(square)
                reach = square * inverse * kappa
                inverse_ref[bead, at, lanes] = inverse
                tallies = [count_ref[s, at, lanes] for s in range(species_count)]
                tally = functools.reduce(jnp.add, tallies)
                sums = list(sums)
                for b in range(basis_count):
                    offset = reach - centers[b]
                    value = jnp.exp2(-(offset * offset))
                    wave_ref[bead, b, at, lanes] = value * offset
                    for s in range(species_count):
                        term = tallies[s] * value
                        sums[b * species_count + s] = sums[b * species_count + s] + (term[:8] + term[8:])
                    if own:
                        high, low = halves(tally * value)
                        high_ref[bead, b, at, lanes] = high
                        low_ref[bead, b, at, lanes] = low
                return tuple(sums)

            zero = jnp.zeros((8, LANES), F32)
            sums = lax.fori_loop(0, extent // ROWS, gather_basis, (zero,) * (basis_count * species_count), unroll=UNROLL)
            for n, total in enumerate(sums):
                start = bead * extent + chunk * LANES
                sums_ref[n * 8 : n * 8 + 8, start : start + LANES] = total

    update = near_dot(first_t_ref[...], sums_ref[...])
    sigmoid = jax.nn.sigmoid(update)
    slope_ref[...] = sigmoid * (1.0 + update * (1.0 - sigmoid))
    hidden = jnp.concatenate([hidden_ref[...]] * reduced_dev, axis=1) + update * sigmoid
    lent_t = near_dot(msg_t_ref[...], hidden)
    lent = lent_t.T
    radial_cols = radial_ref[1].T * scale
    messages = []
    for bead in beads:
        for b in range(basis_count):
            high, low = halves(lent_t[:, bead * extent : (bead + 1) * extent] * radial_cols[:, b : b + 1])
            wide_ref[:channels, b * extent : (b + 1) * extent] = high
            wide_ref[channels:, b * extent : (b + 1) * extent] = low
        both = fast_dot(wide_ref[...], high_ref[bead].reshape(basis_count * extent, atoms))
        last = fast_dot(wide_ref[:channels], low_ref[bead].reshape(basis_count * extent, atoms))
        messages.append(both[:channels] + both[channels:] + last)
    message = jnp.concatenate(messages, axis=1)
    update = near_dot(upd_t_ref[...], message)
    sigmoid = jax.nn.sigmoid(update)
    out_cols = jnp.broadcast_to(out_w_ref[...], (8, channels)).T[:, 0:1]
    grad_update = out_cols * (sigmoid * (1.0 + update * (1.0 - sigmoid)))
    grad_message_t = near_dot(upd_ref[1], grad_update)
    grad_message = grad_message_t.T

    grads_lent = []
    for bead in beads:
        grad_lent = jnp.zeros((extent, channels), F32)
        for b in range(basis_count):
            high, low = halves(grad_message[bead * atoms : (bead + 1) * atoms] * (radial_ref[1, b : b + 1] * scale))
            both = fast_dot(high_ref[bead, b], jnp.concatenate([high, low], axis=1))
            grad_lent = grad_lent + both[:, :channels] + both[:, channels:] + fast_dot(low_ref[bead, b], high)
        grads_lent.append(grad_lent)
    grad_hidden = near_dot(msg_ref[1], jnp.concatenate(grads_lent, axis=0).T)
    parts = []
    for bead in beads:
        start = bead * extent
        parts += [grad_hidden[:, start : start + atoms] + out_cols, grad_hidden[:, start + atoms : start + extent]]
    row_h_ref[...] = near_dot(first_ref[...], jnp.concatenate(parts, axis=1) * slope_ref[...])
    for bead in beads:
        high, low = halves(grad_message_t[:, bead * atoms : (bead + 1) * atoms])
        grads = jnp.concatenate([high, high, low], axis=0)
        for b in range(basis_count):
            high, low = halves(lent[bead * extent : (bead + 1) * extent] * (radial_ref[1, b : b + 1] * scale))
            slope_pair_ref[bead, b] = fast_dot(jnp.concatenate([high, low, high], axis=1), grads)

    pulls = []
    edge_ref[...] = jnp.zeros_like(edge_ref)
    lane_row = lax.broadcasted_iota(jnp.int32, (BLOCK, LANES), 1)
    chain = -2.0 / (radial_width * math.sqrt(math.log2(math.e)))
    for bead in beads:
        for own in (True, False):
            lanes = slice(0, atoms) if own else slice(atoms, extent)
            width = atoms if own else extent - atoms
            start = bead * extent + lanes.start
            here = [ext_own[x * reduced_dev + bead : x * reduced_dev + bead + 1, lanes] for x in range(3)]

            def pair_grads(step, center, bead=bead, lanes=lanes, own=own, width=width, here=here, start=start):
                at = pl.ds(pl.multiple_of(step * BLOCK, BLOCK), BLOCK)
                tallies = [count_ref[s, at, lanes] for s in range(species_count)]
                total = jnp.zeros((BLOCK, width), F32)
                for b in range(basis_count):
                    value = wave_ref[bead, b, at, lanes]

                    def first_layer(s):
                        n = (b * species_count + s) * 8
                        tile = row_h_ref[n : n + 8, start : start + width]
                        return jnp.concatenate([tile] * (BLOCK // 8), axis=0)

                    slope = first_layer(0)
                    for s in range(1, species_count):
                        slope = jnp.where(tallies[s] > 0.0, first_layer(s), slope)
                    if own:
                        slope = slope + slope_pair_ref[bead, b, at, :]
                    total = total + slope * value
                weight = total * functools.reduce(jnp.add, tallies) * inverse_ref[bead, at, lanes] * chain
                center = list(center)
                columns = jnp.zeros((BLOCK, LANES), F32)
                for x in range(3):
                    q = x * reduced_dev + bead
                    place = near(own, q, at)
                    folded = None
                    for chunk in range(width // LANES):
                        cut = slice(chunk * LANES, (chunk + 1) * LANES)
                        pull = weight[:, cut] * (place - here[x][:, cut])
                        folded = pull if folded is None else folded + pull
                        n = x * (width // LANES) + chunk
                        for part in range(BLOCK // 8):
                            center[n] = center[n] + pull[part * 8 : part * 8 + 8]
                    if own:
                        columns = jnp.where(lane_row == q, jnp.sum(folded, axis=1, keepdims=True), columns)
                    else:
                        left = jnp.sum(jnp.where(lane_row < ghosts, folded, 0.0), axis=1, keepdims=True)
                        right = jnp.sum(jnp.where(lane_row < ghosts, 0.0, folded), axis=1, keepdims=True)
                        columns = jnp.where(lane_row == pad_rows + q, left, columns)
                        columns = jnp.where(lane_row == 2 * pad_rows + q, right, columns)
                edge_ref[at, :] = edge_ref[at, :] + columns
                return tuple(center)

            zero = jnp.zeros((8, LANES), F32)
            many = width // LANES
            center = lax.fori_loop(0, extent // BLOCK, pair_grads, (zero,) * (3 * many), unroll=extent // BLOCK)
            pulls.append(
                [
                    jnp.concatenate(
                        [jnp.sum(c, axis=0, keepdims=True) for c in center[x * many : (x + 1) * many]], axis=1
                    )
                    for x in range(3)
                ]
            )

    edges = edge_ref[...].T
    edge_own, edge_left, edge_right = (edges[pad_rows * n : pad_rows * (n + 1)] for n in range(3))
    center = [
        jnp.concatenate([pulls[2 * bead][x], pulls[2 * bead + 1][x]], axis=1) for x in range(3) for bead in beads
    ]
    if rows < pad_rows:
        center.append(jnp.zeros((pad_rows - rows, extent), F32))
    edge_own = edge_own - jnp.concatenate(center, axis=0)

    def at_head(values):
        return jnp.concatenate([values, jnp.zeros((pad_rows, tail), F32)], axis=1)

    def at_tail(values):
        return jnp.concatenate([jnp.zeros((pad_rows, tail), F32), values], axis=1)

    lower = slice(atoms, atoms + ghosts)
    upper = slice(atoms + ghosts, extent)
    back = {
        0: edge_own[:, :atoms] + at_head(edge_left[:, upper]) + at_tail(edge_right[:, lower]),
        -1: edge_left[:, :atoms] + at_tail(edge_own[:, lower]),
        1: edge_right[:, :atoms] + at_head(edge_own[:, upper]),
        -2: at_tail(edge_left[:, lower]),
        2: at_head(edge_right[:, upper]),
    }
    out_ref[0] = jnp.zeros_like(out_ref[0])
    for step, values in back.items():
        place = lax.rem(domain + step + 2 * domains, domains)
        out_ref[0, place] = out_ref[0, place] + values
    for group in range(1, groups):
        out_ref[group] = out_ref[0]


def on_device(
    positions, species, neighbors, counts, send_rows, embed, w_radial, w_msg, w_upd, w_out
):
    full_dev, _, atoms = positions.shape
    groups = lax.axis_size("bead")
    domains = lax.axis_size("space")
    beads_all = full_dev * groups
    reduced_dev = PC // groups
    rows = -(-reduced_dev * 3 // 8) * 8
    slots = neighbors.shape[0]
    ghosts = send_rows.shape[0] // 2
    extent = atoms + 2 * ghosts
    species_count, channels = embed.shape
    layers, basis_count, _ = w_radial.shape
    back_table = collect_table(beads_all, groups, rows)
    vmem = pl.BlockSpec(memory_space=pltpu.VMEM)
    params = pltpu.CompilerParams(vmem_limit_bytes=VMEM_BYTES)

    def shaped(*shape):
        return jax.ShapeDtypeStruct(shape, F32)

    sends = jnp.pad(send_rows, (0, atoms - 2 * ghosts))
    pack = jnp.concatenate([neighbors, counts[None], species[None], sends[None]], axis=0)

    def shift(values, by):
        return lax.ppermute(values, "space", [(i, (i + by) % domains) for i in range(domains)])

    from_left = shift(pack, 1)
    from_right = shift(pack, -1)
    from_far_left = shift(pack, 2)
    from_far_right = from_far_left if domains == 4 else shift(pack, -2)

    spread = pl.pallas_call(
        spread_kernel,
        out_shape=shaped(groups, domains, rows, atoms),
        in_specs=[vmem],
        out_specs=vmem,
        compiler_params=params,
    )(positions.transpose(1, 0, 2))
    arrived = lax.all_to_all(
        spread.reshape(groups * domains, rows, atoms), ("bead", "space"), 0, 0, tiled=True
    )

    sums_rows = basis_count * species_count * 8
    lane_count = 2 * LANES * 3 * reduced_dev
    embed_cols, *weights = pl.pallas_call(
        functools.partial(weights_kernel, slots=slots, ghosts=ghosts),
        out_shape=[
            shaped(channels, 8),
            shaped(sums_rows, channels),
            shaped(channels, sums_rows),
            shaped(channels, channels),
            shaped(channels, channels),
            jax.ShapeDtypeStruct((9 * rows, lane_count), BF16),
        ],
        in_specs=[vmem] * 4,
        out_specs=[vmem] * 6,
        compiler_params=params,
    )(embed, w_radial, w_msg, w_upd)
    prepared = pl.pallas_call(
        functools.partial(counts_kernel, slots=slots, ghosts=ghosts),
        out_shape=[shaped(species_count, extent, extent), shaped(channels, extent)],
        in_specs=[vmem] * 6,
        out_specs=[vmem] * 2,
        compiler_params=params,
    )(pack, from_left, from_right, from_far_left, from_far_right, embed_cols)

    grads = pl.pallas_call(
        functools.partial(force_kernel, domains=domains, slots=slots, ghosts=ghosts, reduced_dev=reduced_dev),
        out_shape=shaped(groups, domains, rows, atoms),
        in_specs=[vmem] * 12,
        out_specs=vmem,
        scratch_shapes=[
            pltpu.VMEM((extent, lane_count), F32),
            pltpu.VMEM((reduced_dev, extent, extent), F32),
            pltpu.VMEM((reduced_dev, basis_count, extent, atoms), BF16),
            pltpu.VMEM((reduced_dev, basis_count, extent, atoms), BF16),
            pltpu.VMEM((sums_rows, reduced_dev * extent), F32),
            pltpu.VMEM((extent, LANES), F32),
            pltpu.VMEM((reduced_dev, basis_count, extent, atoms), F32),
            pltpu.VMEM((channels, reduced_dev * extent), F32),
            pltpu.VMEM((sums_rows, reduced_dev * extent), F32),
            pltpu.VMEM((2 * channels, basis_count * extent), BF16),
            pltpu.VMEM((reduced_dev, basis_count, extent, extent), F32),
        ],
        compiler_params=params,
    )(arrived, *prepared, *weights, w_radial, w_msg, w_upd, w_out[None])

    returned = lax.all_to_all(
        grads.reshape(groups * domains, rows, atoms), ("bead", "space"), 0, 0, tiled=True
    )
    forces = pl.pallas_call(
        collect_kernel,
        out_shape=shaped(3, full_dev, atoms),
        in_specs=[vmem, vmem],
        out_specs=vmem,
        compiler_params=params,
    )(back_table, returned.reshape(groups, domains, rows, atoms))
    return forces.transpose(1, 0, 2)


def solution(mesh):
    return jax.shard_map(
        on_device,
        mesh=mesh,
        in_specs=(
            P("bead", None, "space"),
            P("space"),
            P(None, "space"),
            P("space"),
            P("space"),
            P(),
            P(),
            P(),
            P(),
            P(),
        ),
        out_specs=P("bead", None, "space"),
        check_vma=False,
    )
```

```python
import functools
import math

import jax
import jax.numpy as jnp
import numpy as np
from jax import lax
from jax.experimental import pallas as pl
from jax.experimental.pallas import tpu as pltpu
from jax.sharding import PartitionSpec as P

PC = 16

exact_mode = lax.Precision.HIGHEST
spacing_floor = 0.01
radial_width = 0.2
radial_reach = 1.5
LANES = 128
PLANES = 4
ROWS = 16
BLOCK = 64
F32 = jnp.float32
BF16 = jnp.bfloat16
UNROLL = 24
VMEM_BYTES = 48 * 1024 * 1024
kappa = math.sqrt(math.log2(math.e)) / radial_width


def contraction(full_beads, reduced_beads):
    gap = np.arange(reduced_beads)[:, None] / reduced_beads - np.arange(full_beads)[None, :] / full_beads
    total = np.ones_like(gap)
    for harmonic in range(1, reduced_beads // 2):
        total = total + 2.0 * np.cos(2.0 * np.pi * harmonic * gap)
    total = total + np.cos(np.pi * reduced_beads * gap)
    return (total / full_beads).astype(np.float32)


def exact_dot(left, right):
    return lax.dot(left, right, precision=exact_mode, preferred_element_type=F32)


def near_dot(left, right):
    return lax.dot(left, right, precision=lax.Precision.HIGH, preferred_element_type=F32)


def fast_dot(left, right):
    return lax.dot(left, right, preferred_element_type=F32)


def halves(values):
    high = values.astype(BF16)
    low = (values - high.astype(F32)).astype(BF16)
    return high, low


def spread_kernel(pos_ref, out_ref):
    components, full_dev, atoms = pos_ref.shape
    groups, domains, reduced_dev, _ = out_ref.shape
    beads_all = groups * full_dev
    k = lax.broadcasted_iota(jnp.int32, (PC, full_dev), 0).astype(F32)
    j = lax.broadcasted_iota(jnp.int32, (PC, full_dev), 1) + lax.axis_index("bead") * full_dev
    gap = k / PC - j.astype(F32) / beads_all
    table = jnp.ones_like(gap)
    for harmonic in range(1, PC // 2 + 1):
        turn = gap * harmonic
        wave = jnp.cos((turn - jnp.floor(turn)) * (2.0 * math.pi))
        table = table + (wave if harmonic == PC // 2 else 2.0 * wave)
    table = table / beads_all
    total = exact_dot(table, jnp.concatenate([pos_ref[x] for x in range(components)], axis=1))
    for group in range(groups):
        block = total[group * reduced_dev : (group + 1) * reduced_dev]
        for domain in range(domains):
            out_ref[group, domain] = block


def collect_kernel(table_ref, in_ref, out_ref):
    groups, domains = in_ref.shape[:2]
    atoms = out_ref.shape[2]
    pulls = []
    for group in range(groups):
        total = in_ref[group, 0]
        for domain in range(1, domains):
            total = total + in_ref[group, domain]
        pulls.append(total)
    out = exact_dot(table_ref[lax.axis_index("bead")], jnp.concatenate(pulls, axis=0))
    for x in range(out_ref.shape[0]):
        out_ref[x] = out[:, x * atoms : (x + 1) * atoms]


def collect_table(beads_all, groups):
    table = contraction(beads_all, PC).T.reshape(groups, beads_all // groups, PC)
    return jnp.asarray(-(beads_all / PC) * table)


def weights_kernel(
    embed_ref, radial_ref, msg_ref, upd_ref,
    embed_cols_ref, first_ref, first_t_ref, msg_t_ref, upd_t_ref, fan_ref,
    *, slots, ghosts,
):
    species_count, channels = embed_ref.shape
    basis_count = radial_ref.shape[1]
    embed = embed_ref[...]
    embed_pad = jnp.concatenate([embed, jnp.zeros((8 - species_count, channels), F32)], axis=0)
    embed_cols_ref[...] = embed_pad.T
    scale = slots ** (-0.5)
    lent = exact_dot(embed_pad, msg_ref[0])
    stacked = []
    for b in range(basis_count):
        for s in range(species_count):
            row = radial_ref[0, b : b + 1] * lent[s : s + 1] * scale
            stacked.append(jnp.broadcast_to(row, (8, channels)))
    first = exact_dot(jnp.concatenate(stacked, axis=0), upd_ref[0])
    first_ref[...] = first
    first_t_ref[...] = first.T
    msg_t_ref[...] = msg_ref[1].T
    upd_t_ref[...] = upd_ref[1].T

    row = lax.broadcasted_iota(jnp.int32, fan_ref.shape, 0)
    column = lax.broadcasted_iota(jnp.int32, fan_ref.shape, 1)
    part = lax.rem(column, 2 * LANES)
    part = (part >= LANES).astype(jnp.int32) + (part >= LANES + ghosts).astype(jnp.int32)
    pad_rows = fan_ref.shape[0] // 9
    fan_ref[...] = jnp.where(
        lax.rem(row, 3 * pad_rows) == part * pad_rows + lax.div(column, 2 * LANES), 1.0, 0.0
    ).astype(BF16)


def counts_kernel(
    own_ref, left_ref, right_ref, far_left_ref, far_right_ref, embed_cols_ref, count_ref, hidden_ref, *, slots, ghosts
):
    atoms = own_ref.shape[1]
    channels = embed_cols_ref.shape[0]
    species_count = count_ref.shape[0]
    extent = atoms + 2 * ghosts
    tail = atoms - ghosts
    count_row, species_row, send_row = slots, slots + 1, slots + 2

    def edge_pack(row, rows=1):
        return jnp.concatenate(
            [own_ref[row : row + rows], left_ref[row : row + rows, tail:], right_ref[row : row + rows, :ghosts]],
            axis=1,
        )

    neighbors = edge_pack(0, slots)
    counts = edge_pack(count_row)
    own_send = own_ref[send_row : send_row + 1]
    left_send = left_ref[send_row : send_row + 1]
    right_send = right_ref[send_row : send_row + 1]
    far_left_send = far_left_ref[send_row : send_row + 1]
    far_right_send = far_right_ref[send_row : send_row + 1]

    def ghost_map(from_left, from_right):
        return jnp.concatenate(
            [from_left[:, ghosts : 2 * ghosts] - tail, from_right[:, :ghosts] + ghosts], axis=1
        )

    maps = [
        ghost_map(left_send, right_send),
        ghost_map(far_left_send, own_send),
        ghost_map(own_send, far_right_send),
    ]
    maps = [jnp.broadcast_to(m, (slots, 2 * ghosts)) for m in maps]
    lane = lax.broadcasted_iota(jnp.int32, (slots, LANES), 1)
    slot = lax.broadcasted_iota(jnp.int32, (slots, LANES), 0)

    species_rows = []
    for near, lower, upper in (
        (own_ref[species_row : species_row + 1], left_ref[species_row : species_row + 1], right_ref[species_row : species_row + 1]),
        (left_ref[species_row : species_row + 1], far_left_ref[species_row : species_row + 1], own_ref[species_row : species_row + 1]),
        (right_ref[species_row : species_row + 1], own_ref[species_row : species_row + 1], far_right_ref[species_row : species_row + 1]),
    ):
        species_rows.append(jnp.concatenate([near, lower[:, tail:], upper[:, :ghosts]], axis=1))
    species_f = jnp.concatenate(species_rows + [species_rows[0]] * 5, axis=0).astype(F32)
    species_cols = species_f.T

    plane_rows = extent // PLANES
    chunks = extent // LANES
    plane_iota = lax.broadcasted_iota(jnp.int32, (plane_rows, LANES), 0)
    lane_block = lax.broadcasted_iota(jnp.int32, (plane_rows, LANES), 1)
    for chunk in range(chunks):
        lanes = slice(chunk * LANES, (chunk + 1) * LANES)
        rows_now = neighbors[:, lanes]
        index = jnp.clip(rows_now - atoms, 0, 2 * ghosts - 1)
        if (chunk + 1) * LANES <= atoms:
            mapped = jnp.take_along_axis(maps[0], index, axis=1, mode="promise_in_bounds")
        else:
            mapped = jnp.where(
                lane < ghosts,
                jnp.take_along_axis(maps[1], index, axis=1, mode="promise_in_bounds"),
                jnp.take_along_axis(maps[2], index, axis=1, mode="promise_in_bounds"),
            )
        rows_now = jnp.where(rows_now >= atoms, atoms + mapped, rows_now)
        plane = jnp.zeros_like(rows_now)
        for step in range(1, PLANES):
            plane = plane + (rows_now >= step * plane_rows).astype(jnp.int32)
        within = rows_now - plane * plane_rows
        within = jnp.where(slot < counts[:, lanes], within, -1)
        value = jnp.left_shift(jnp.ones_like(plane), 8 * plane)
        words = jnp.zeros((plane_rows, LANES), jnp.int32)
        for k in range(slots):
            words = words + jnp.where(within[k : k + 1] == plane_iota, value[k : k + 1], 0)
        for step in range(PLANES):
            rows = slice(step * plane_rows, (step + 1) * plane_rows)
            tally = (jnp.right_shift(words, 8 * step) & 255).astype(F32)
            if (chunk + 1) * LANES <= atoms:
                kind = jnp.broadcast_to(species_cols[rows, 0:1], (plane_rows, LANES))
            else:
                kind = jnp.where(lane_block < ghosts, species_cols[rows, 1:2], species_cols[rows, 2:3])
            for s in range(species_count):
                count_ref[s, rows, lanes] = jnp.where(kind == float(s), tally, 0.0)

    hidden = jnp.zeros((channels, extent), F32)
    for s in range(species_count):
        hidden = hidden + embed_cols_ref[:, s : s + 1] * (species_f[0:1] == float(s)).astype(F32)
    hidden_ref[...] = hidden


def force_kernel(
    recv_ref, count_ref, hidden_ref, first_ref, first_t_ref, msg_t_ref, upd_t_ref, fan_ref, radial_ref, msg_ref, upd_ref, out_w_ref,
    out_ref,
    near_ref, inverse_ref, high_ref, low_ref, sums_ref, edge_ref, slope_pair_ref, slope_ref, row_h_ref, wide_ref, wave_ref,
    *, domains, slots, ghosts, reduced_dev,
):
    groups = recv_ref.shape[0] // domains
    rows = reduced_dev * 3
    pad_rows = -(-rows // 8) * 8
    atoms = recv_ref.shape[2] // 3
    extent = atoms + 2 * ghosts
    tail = atoms - ghosts
    species_count = count_ref.shape[0]
    basis_count, channels = radial_ref.shape[1:]
    own_chunks = atoms // LANES
    chunks = extent // LANES
    beads = range(reduced_dev)
    domain = lax.axis_index("space")
    scale = slots ** (-0.5)
    centers = [kappa * radial_reach * b / (basis_count - 1) for b in range(basis_count)]

    is_first = lax.broadcasted_iota(jnp.int32, (pad_rows, atoms), 0) < reduced_dev
    segment = {}
    for step in range(-2, 3):
        shifted = domain + step + 2 * domains
        place = lax.rem(shifted, domains)
        wraps = (lax.div(shifted, domains) - 2).astype(F32) * float(domains)
        total = recv_ref[place]
        for group in range(1, groups):
            total = total + recv_ref[group * domains + place]
        total = [total[:, x * atoms : (x + 1) * atoms] for x in range(3)]
        if rows < pad_rows:
            total.append(jnp.zeros((pad_rows - rows, atoms), F32))
        total = jnp.concatenate(total, axis=0)
        segment[step] = total + jnp.where(is_first, wraps, 0.0)

    def extended(step):
        return jnp.concatenate(
            [segment[step], segment[step - 1][:, tail:], segment[step + 1][:, :ghosts]], axis=1
        )

    ext_own, ext_left, ext_right = extended(0), extended(-1), extended(1)
    stacked = jnp.concatenate([ext_own, ext_left, ext_right], axis=0)
    high = stacked.astype(BF16).astype(F32)
    middle = (stacked - high).astype(BF16).astype(F32)
    parts = jnp.concatenate([high, middle, stacked - high - middle], axis=0)
    near_ref[...] = fast_dot(parts.T.astype(BF16), fan_ref[...])

    def near(own, q, at):
        start = (2 * q + (0 if own else 1)) * LANES
        return near_ref[at, start : start + LANES]


    for bead in beads:
        for chunk in range(chunks):
            lanes = slice(chunk * LANES, (chunk + 1) * LANES)
            own = chunk < own_chunks
            here = [
                jnp.broadcast_to(ext_own[x * reduced_dev + bead : x * reduced_dev + bead + 1, lanes], (ROWS, LANES))
                for x in range(3)
            ]

            def gather_basis(step, sums, bead=bead, lanes=lanes, own=own, here=here):
                at = pl.ds(pl.multiple_of(step * ROWS, ROWS), ROWS)
                square = spacing_floor
                for x in range(3):
                    delta = near(own, x * reduced_dev + bead, at) - here[x]
                    square = square + delta * delta
                inverse = lax.rsqrt(square)
                reach = square * inverse * kappa
                inverse_ref[bead, at, lanes] = inverse
                tallies = [count_ref[s, at, lanes] for s in range(species_count)]
                tally = functools.reduce(jnp.add, tallies)
                sums = list(sums)
                for b in range(basis_count):
                    offset = reach - centers[b]
                    value = jnp.exp2(-(offset * offset))
                    wave_ref[bead, b, at, lanes] = value * offset
                    for s in range(species_count):
                        term = tallies[s] * value
                        sums[b * species_count + s] = sums[b * species_count + s] + (term[:8] + term[8:])
                    if own:
                        high, low = halves(tally * value)
                        high_ref[bead, b, at, lanes] = high
                        low_ref[bead, b, at, lanes] = low
                return tuple(sums)

            zero = jnp.zeros((8, LANES), F32)
            sums = lax.fori_loop(0, extent // ROWS, gather_basis, (zero,) * (basis_count * species_count), unroll=UNROLL)
            for n, total in enumerate(sums):
                start = bead * extent + chunk * LANES
                sums_ref[n * 8 : n * 8 + 8, start : start + LANES] = total

    update = near_dot(first_t_ref[...], sums_ref[...])
    sigmoid = jax.nn.sigmoid(update)
    slope_ref[...] = sigmoid * (1.0 + update * (1.0 - sigmoid))
    hidden = jnp.concatenate([hidden_ref[...]] * reduced_dev, axis=1) + update * sigmoid
    lent_t = near_dot(msg_t_ref[...], hidden)
    lent = lent_t.T
    radial_cols = radial_ref[1].T * scale
    messages = []
    for bead in beads:
        for b in range(basis_count):
            high, low = halves(lent_t[:, bead * extent : (bead + 1) * extent] * radial_cols[:, b : b + 1])
            wide_ref[:channels, b * extent : (b + 1) * extent] = high
            wide_ref[channels:, b * extent : (b + 1) * extent] = low
        both = fast_dot(wide_ref[...], high_ref[bead].reshape(basis_count * extent, atoms))
        last = fast_dot(wide_ref[:channels], low_ref[bead].reshape(basis_count * extent, atoms))
        messages.append(both[:channels] + both[channels:] + last)
    message = jnp.concatenate(messages, axis=1)
    update = near_dot(upd_t_ref[...], message)
    sigmoid = jax.nn.sigmoid(update)
    out_cols = jnp.broadcast_to(out_w_ref[...], (8, channels)).T[:, 0:1]
    grad_update = out_cols * (sigmoid * (1.0 + update * (1.0 - sigmoid)))
    grad_message_t = near_dot(upd_ref[1], grad_update)
    grad_message = grad_message_t.T

    grads_lent = []
    for bead in beads:
        grad_lent = jnp.zeros((extent, channels), F32)
        for b in range(basis_count):
            high, low = halves(grad_message[bead * atoms : (bead + 1) * atoms] * (radial_ref[1, b : b + 1] * scale))
            both = fast_dot(high_ref[bead, b], jnp.concatenate([high, low], axis=1))
            grad_lent = grad_lent + both[:, :channels] + both[:, channels:] + fast_dot(low_ref[bead, b], high)
        grads_lent.append(grad_lent)
    grad_hidden = near_dot(msg_ref[1], jnp.concatenate(grads_lent, axis=0).T)
    parts = []
    for bead in beads:
        start = bead * extent
        parts += [grad_hidden[:, start : start + atoms] + out_cols, grad_hidden[:, start + atoms : start + extent]]
    row_h_ref[...] = near_dot(first_ref[...], jnp.concatenate(parts, axis=1) * slope_ref[...])
    for bead in beads:
        high, low = halves(grad_message_t[:, bead * atoms : (bead + 1) * atoms])
        grads = jnp.concatenate([high, high, low], axis=0)
        for b in range(basis_count):
            high, low = halves(lent[bead * extent : (bead + 1) * extent] * (radial_ref[1, b : b + 1] * scale))
            slope_pair_ref[bead, b] = fast_dot(jnp.concatenate([high, low, high], axis=1), grads)

    pulls = []
    edge_ref[...] = jnp.zeros_like(edge_ref)
    lane_row = lax.broadcasted_iota(jnp.int32, (BLOCK, LANES), 1)
    chain = -2.0 / (radial_width * math.sqrt(math.log2(math.e)))
    for bead in beads:
        for own in (True, False):
            lanes = slice(0, atoms) if own else slice(atoms, extent)
            width = atoms if own else extent - atoms
            start = bead * extent + lanes.start
            here = [ext_own[x * reduced_dev + bead : x * reduced_dev + bead + 1, lanes] for x in range(3)]

            def pair_grads(step, center, bead=bead, lanes=lanes, own=own, width=width, here=here, start=start):
                at = pl.ds(pl.multiple_of(step * BLOCK, BLOCK), BLOCK)
                tallies = [count_ref[s, at, lanes] for s in range(species_count)]
                total = jnp.zeros((BLOCK, width), F32)
                for b in range(basis_count):
                    value = wave_ref[bead, b, at, lanes]

                    def first_layer(s):
                        n = (b * species_count + s) * 8
                        tile = row_h_ref[n : n + 8, start : start + width]
                        return jnp.concatenate([tile] * (BLOCK // 8), axis=0)

                    slope = first_layer(0)
                    for s in range(1, species_count):
                        slope = jnp.where(tallies[s] > 0.0, first_layer(s), slope)
                    if own:
                        slope = slope + slope_pair_ref[bead, b, at, :]
                    total = total + slope * value
                weight = total * functools.reduce(jnp.add, tallies) * inverse_ref[bead, at, lanes] * chain
                center = list(center)
                columns = jnp.zeros((BLOCK, LANES), F32)
                for x in range(3):
                    q = x * reduced_dev + bead
                    place = near(own, q, at)
                    folded = None
                    for chunk in range(width // LANES):
                        cut = slice(chunk * LANES, (chunk + 1) * LANES)
                        pull = weight[:, cut] * (place - here[x][:, cut])
                        folded = pull if folded is None else folded + pull
                        n = x * (width // LANES) + chunk
                        for part in range(BLOCK // 8):
                            center[n] = center[n] + pull[part * 8 : part * 8 + 8]
                    if own:
                        columns = jnp.where(lane_row == q, jnp.sum(folded, axis=1, keepdims=True), columns)
                    else:
                        left = jnp.sum(jnp.where(lane_row < ghosts, folded, 0.0), axis=1, keepdims=True)
                        right = jnp.sum(jnp.where(lane_row < ghosts, 0.0, folded), axis=1, keepdims=True)
                        columns = jnp.where(lane_row == pad_rows + q, left, columns)
                        columns = jnp.where(lane_row == 2 * pad_rows + q, right, columns)
                edge_ref[at, :] = edge_ref[at, :] + columns
                return tuple(center)

            zero = jnp.zeros((8, LANES), F32)
            many = width // LANES
            center = lax.fori_loop(0, extent // BLOCK, pair_grads, (zero,) * (3 * many), unroll=extent // BLOCK)
            pulls.append(
                [
                    jnp.concatenate(
                        [jnp.sum(c, axis=0, keepdims=True) for c in center[x * many : (x + 1) * many]], axis=1
                    )
                    for x in range(3)
                ]
            )

    edges = edge_ref[...].T
    edge_own, edge_left, edge_right = (edges[pad_rows * n : pad_rows * (n + 1)] for n in range(3))
    center = [
        jnp.concatenate([pulls[2 * bead][x], pulls[2 * bead + 1][x]], axis=1) for x in range(3) for bead in beads
    ]
    if rows < pad_rows:
        center.append(jnp.zeros((pad_rows - rows, extent), F32))
    edge_own = edge_own - jnp.concatenate(center, axis=0)

    def at_head(values):
        return jnp.concatenate([values, jnp.zeros((pad_rows, tail), F32)], axis=1)

    def at_tail(values):
        return jnp.concatenate([jnp.zeros((pad_rows, tail), F32), values], axis=1)

    lower = slice(atoms, atoms + ghosts)
    upper = slice(atoms + ghosts, extent)
    back = {
        0: edge_own[:, :atoms] + at_head(edge_left[:, upper]) + at_tail(edge_right[:, lower]),
        -1: edge_left[:, :atoms] + at_tail(edge_own[:, lower]),
        1: edge_right[:, :atoms] + at_head(edge_own[:, upper]),
        -2: at_tail(edge_left[:, lower]),
        2: at_head(edge_right[:, upper]),
    }
    out_ref[0] = jnp.zeros_like(out_ref[0])
    for step, values in back.items():
        place = lax.rem(domain + step + 2 * domains, domains)
        flat = [values[x * reduced_dev : (x + 1) * reduced_dev] for x in range(3)]
        out_ref[0, place] = out_ref[0, place] + jnp.concatenate(flat, axis=1)
    for group in range(1, groups):
        out_ref[group] = out_ref[0]


def on_device(
    positions, species, neighbors, counts, send_rows, embed, w_radial, w_msg, w_upd, w_out
):
    full_dev, _, atoms = positions.shape
    groups = lax.axis_size("bead")
    domains = lax.axis_size("space")
    beads_all = full_dev * groups
    reduced_dev = PC // groups
    rows = -(-reduced_dev * 3 // 8) * 8
    slots = neighbors.shape[0]
    ghosts = send_rows.shape[0] // 2
    extent = atoms + 2 * ghosts
    species_count, channels = embed.shape
    layers, basis_count, _ = w_radial.shape
    back_table = collect_table(beads_all, groups)
    vmem = pl.BlockSpec(memory_space=pltpu.VMEM)
    params = pltpu.CompilerParams(vmem_limit_bytes=VMEM_BYTES)

    def shaped(*shape):
        return jax.ShapeDtypeStruct(shape, F32)

    sends = jnp.pad(send_rows, (0, atoms - 2 * ghosts))
    pack = jnp.concatenate([neighbors, counts[None], species[None], sends[None]], axis=0)

    def shift(values, by):
        return lax.ppermute(values, "space", [(i, (i + by) % domains) for i in range(domains)])

    from_left = shift(pack, 1)
    from_right = shift(pack, -1)
    from_far_left = shift(pack, 2)
    from_far_right = from_far_left if domains == 4 else shift(pack, -2)

    spread = pl.pallas_call(
        spread_kernel,
        out_shape=shaped(groups, domains, reduced_dev, 3 * atoms),
        in_specs=[vmem],
        out_specs=vmem,
        compiler_params=params,
    )(positions.transpose(1, 0, 2))
    arrived = lax.all_to_all(
        spread.reshape(groups * domains, reduced_dev, 3 * atoms), ("bead", "space"), 0, 0, tiled=True
    )

    sums_rows = basis_count * species_count * 8
    lane_count = 2 * LANES * 3 * reduced_dev
    embed_cols, *weights = pl.pallas_call(
        functools.partial(weights_kernel, slots=slots, ghosts=ghosts),
        out_shape=[
            shaped(channels, 8),
            shaped(sums_rows, channels),
            shaped(channels, sums_rows),
            shaped(channels, channels),
            shaped(channels, channels),
            jax.ShapeDtypeStruct((9 * rows, lane_count), BF16),
        ],
        in_specs=[vmem] * 4,
        out_specs=[vmem] * 6,
        compiler_params=params,
    )(embed, w_radial, w_msg, w_upd)
    prepared = pl.pallas_call(
        functools.partial(counts_kernel, slots=slots, ghosts=ghosts),
        out_shape=[shaped(species_count, extent, extent), shaped(channels, extent)],
        in_specs=[vmem] * 6,
        out_specs=[vmem] * 2,
        compiler_params=params,
    )(pack, from_left, from_right, from_far_left, from_far_right, embed_cols)

    grads = pl.pallas_call(
        functools.partial(force_kernel, domains=domains, slots=slots, ghosts=ghosts, reduced_dev=reduced_dev),
        out_shape=shaped(groups, domains, reduced_dev, 3 * atoms),
        in_specs=[vmem] * 12,
        out_specs=vmem,
        scratch_shapes=[
            pltpu.VMEM((extent, lane_count), F32),
            pltpu.VMEM((reduced_dev, extent, extent), F32),
            pltpu.VMEM((reduced_dev, basis_count, extent, atoms), BF16),
            pltpu.VMEM((reduced_dev, basis_count, extent, atoms), BF16),
            pltpu.VMEM((sums_rows, reduced_dev * extent), F32),
            pltpu.VMEM((extent, LANES), F32),
            pltpu.VMEM((reduced_dev, basis_count, extent, atoms), F32),
            pltpu.VMEM((channels, reduced_dev * extent), F32),
            pltpu.VMEM((sums_rows, reduced_dev * extent), F32),
            pltpu.VMEM((2 * channels, basis_count * extent), BF16),
            pltpu.VMEM((reduced_dev, basis_count, extent, extent), F32),
        ],
        compiler_params=params,
    )(arrived, *prepared, *weights, w_radial, w_msg, w_upd, w_out[None])

    returned = lax.all_to_all(
        grads.reshape(groups * domains, reduced_dev, 3 * atoms), ("bead", "space"), 0, 0, tiled=True
    )
    forces = pl.pallas_call(
        collect_kernel,
        out_shape=shaped(3, full_dev, atoms),
        in_specs=[vmem, vmem],
        out_specs=vmem,
        compiler_params=params,
    )(back_table, returned.reshape(groups, domains, reduced_dev, 3 * atoms))
    return forces.transpose(1, 0, 2)


def solution(mesh):
    return jax.shard_map(
        on_device,
        mesh=mesh,
        in_specs=(
            P("bead", None, "space"),
            P("space"),
            P(None, "space"),
            P("space"),
            P("space"),
            P(),
            P(),
            P(),
            P(),
            P(),
        ),
        out_specs=P("bead", None, "space"),
        check_vma=False,
    )
```

```python
import functools
import math

import jax
import jax.numpy as jnp
import numpy as np
from jax import lax
from jax.experimental import pallas as pl
from jax.experimental.pallas import tpu as pltpu
from jax.sharding import PartitionSpec as P

PC = 16

exact_mode = lax.Precision.HIGHEST
spacing_floor = 0.01
radial_width = 0.2
radial_reach = 1.5
LANES = 128
PLANES = 4
ROWS = 16
BLOCK = 64
F32 = jnp.float32
BF16 = jnp.bfloat16
UNROLL = 24
VMEM_BYTES = 48 * 1024 * 1024
kappa = math.sqrt(math.log2(math.e)) / radial_width


def contraction(full_beads, reduced_beads):
    gap = np.arange(reduced_beads)[:, None] / reduced_beads - np.arange(full_beads)[None, :] / full_beads
    total = np.ones_like(gap)
    for harmonic in range(1, reduced_beads // 2):
        total = total + 2.0 * np.cos(2.0 * np.pi * harmonic * gap)
    total = total + np.cos(np.pi * reduced_beads * gap)
    return (total / full_beads).astype(np.float32)


def exact_dot(left, right):
    return lax.dot(left, right, precision=exact_mode, preferred_element_type=F32)


def near_dot(left, right):
    return lax.dot(left, right, precision=lax.Precision.HIGH, preferred_element_type=F32)


def fast_dot(left, right):
    return lax.dot(left, right, preferred_element_type=F32)


def halves(values):
    high = values.astype(BF16)
    low = (values - high.astype(F32)).astype(BF16)
    return high, low


def spread_kernel(pos_ref, out_ref):
    components, full_dev, atoms = pos_ref.shape
    groups, domains, reduced_dev, _ = out_ref.shape
    beads_all = groups * full_dev
    k = lax.broadcasted_iota(jnp.int32, (PC, full_dev), 0).astype(F32)
    j = lax.broadcasted_iota(jnp.int32, (PC, full_dev), 1) + lax.axis_index("bead") * full_dev
    gap = k / PC - j.astype(F32) / beads_all
    table = jnp.ones_like(gap)
    for harmonic in range(1, PC // 2 + 1):
        turn = gap * harmonic
        wave = jnp.cos((turn - jnp.floor(turn)) * (2.0 * math.pi))
        table = table + (wave if harmonic == PC // 2 else 2.0 * wave)
    table = table / beads_all
    total = exact_dot(table, jnp.concatenate([pos_ref[x] for x in range(components)], axis=1))
    for group in range(groups):
        block = total[group * reduced_dev : (group + 1) * reduced_dev]
        for domain in range(domains):
            out_ref[group, domain] = block


def collect_kernel(table_ref, in_ref, out_ref):
    groups, domains = in_ref.shape[:2]
    atoms = out_ref.shape[2]
    pulls = []
    for group in range(groups):
        total = in_ref[group, 0]
        for domain in range(1, domains):
            total = total + in_ref[group, domain]
        pulls.append(total)
    out = exact_dot(table_ref[lax.axis_index("bead")], jnp.concatenate(pulls, axis=0))
    for x in range(out_ref.shape[0]):
        out_ref[x] = out[:, x * atoms : (x + 1) * atoms]


def collect_table(beads_all, groups):
    table = contraction(beads_all, PC).T.reshape(groups, beads_all // groups, PC)
    return jnp.asarray(-(beads_all / PC) * table)


def weights_kernel(
    embed_ref, radial_ref, msg_ref, upd_ref,
    embed_cols_ref, first_ref, first_t_ref, msg_t_ref, upd_t_ref, fan_ref, last_radial_ref, last_msg_ref, last_upd_ref,
    *, slots, ghosts,
):
    species_count, channels = embed_ref.shape
    basis_count = radial_ref.shape[1]
    embed = embed_ref[...]
    embed_pad = jnp.concatenate([embed, jnp.zeros((8 - species_count, channels), F32)], axis=0)
    embed_cols_ref[...] = embed_pad.T
    scale = slots ** (-0.5)
    lent = exact_dot(embed_pad, msg_ref[0])
    stacked = []
    for b in range(basis_count):
        for s in range(species_count):
            row = radial_ref[0, b : b + 1] * lent[s : s + 1] * scale
            stacked.append(jnp.broadcast_to(row, (8, channels)))
    first = exact_dot(jnp.concatenate(stacked, axis=0), upd_ref[0])
    first_ref[...] = first
    first_t_ref[...] = first.T
    msg_t_ref[...] = msg_ref[1].T
    upd_t_ref[...] = upd_ref[1].T
    last_radial_ref[...] = radial_ref[1]
    last_msg_ref[...] = msg_ref[1]
    last_upd_ref[...] = upd_ref[1]

    row = lax.broadcasted_iota(jnp.int32, fan_ref.shape, 0)
    column = lax.broadcasted_iota(jnp.int32, fan_ref.shape, 1)
    part = lax.rem(column, 2 * LANES)
    part = (part >= LANES).astype(jnp.int32) + (part >= LANES + ghosts).astype(jnp.int32)
    pad_rows = fan_ref.shape[0] // 9
    fan_ref[...] = jnp.where(
        lax.rem(row, 3 * pad_rows) == part * pad_rows + lax.div(column, 2 * LANES), 1.0, 0.0
    ).astype(BF16)


def counts_kernel(
    own_ref, left_ref, right_ref, far_left_ref, far_right_ref, embed_cols_ref, count_ref, hidden_ref, *, slots, ghosts
):
    atoms = own_ref.shape[1]
    channels = embed_cols_ref.shape[0]
    species_count = count_ref.shape[0]
    extent = atoms + 2 * ghosts
    tail = atoms - ghosts
    count_row, species_row, send_row = slots, slots + 1, slots + 2

    def edge_pack(row, rows=1):
        return jnp.concatenate(
            [own_ref[row : row + rows], left_ref[row : row + rows, tail:], right_ref[row : row + rows, :ghosts]],
            axis=1,
        )

    neighbors = edge_pack(0, slots)
    counts = edge_pack(count_row)
    own_send = own_ref[send_row : send_row + 1]
    left_send = left_ref[send_row : send_row + 1]
    right_send = right_ref[send_row : send_row + 1]
    far_left_send = far_left_ref[send_row : send_row + 1]
    far_right_send = far_right_ref[send_row : send_row + 1]

    def ghost_map(from_left, from_right):
        return jnp.concatenate(
            [from_left[:, ghosts : 2 * ghosts] - tail, from_right[:, :ghosts] + ghosts], axis=1
        )

    maps = [
        ghost_map(left_send, right_send),
        ghost_map(far_left_send, own_send),
        ghost_map(own_send, far_right_send),
    ]
    maps = [jnp.broadcast_to(m, (slots, 2 * ghosts)) for m in maps]
    lane = lax.broadcasted_iota(jnp.int32, (slots, LANES), 1)
    slot = lax.broadcasted_iota(jnp.int32, (slots, LANES), 0)

    species_rows = []
    for near, lower, upper in (
        (own_ref[species_row : species_row + 1], left_ref[species_row : species_row + 1], right_ref[species_row : species_row + 1]),
        (left_ref[species_row : species_row + 1], far_left_ref[species_row : species_row + 1], own_ref[species_row : species_row + 1]),
        (right_ref[species_row : species_row + 1], own_ref[species_row : species_row + 1], far_right_ref[species_row : species_row + 1]),
    ):
        species_rows.append(jnp.concatenate([near, lower[:, tail:], upper[:, :ghosts]], axis=1))
    species_f = jnp.concatenate(species_rows + [species_rows[0]] * 5, axis=0).astype(F32)
    species_cols = species_f.T

    plane_rows = extent // PLANES
    chunks = extent // LANES
    plane_iota = lax.broadcasted_iota(jnp.int32, (plane_rows, LANES), 0)
    lane_block = lax.broadcasted_iota(jnp.int32, (plane_rows, LANES), 1)
    for chunk in range(chunks):
        lanes = slice(chunk * LANES, (chunk + 1) * LANES)
        rows_now = neighbors[:, lanes]
        index = jnp.clip(rows_now - atoms, 0, 2 * ghosts - 1)
        if (chunk + 1) * LANES <= atoms:
            mapped = jnp.take_along_axis(maps[0], index, axis=1, mode="promise_in_bounds")
        else:
            mapped = jnp.where(
                lane < ghosts,
                jnp.take_along_axis(maps[1], index, axis=1, mode="promise_in_bounds"),
                jnp.take_along_axis(maps[2], index, axis=1, mode="promise_in_bounds"),
            )
        rows_now = jnp.where(rows_now >= atoms, atoms + mapped, rows_now)
        plane = jnp.zeros_like(rows_now)
        for step in range(1, PLANES):
            plane = plane + (rows_now >= step * plane_rows).astype(jnp.int32)
        within = rows_now - plane * plane_rows
        within = jnp.where(slot < counts[:, lanes], within, -1)
        value = jnp.left_shift(jnp.ones_like(plane), 8 * plane)
        words = jnp.zeros((plane_rows, LANES), jnp.int32)
        for k in range(slots):
            words = words + jnp.where(within[k : k + 1] == plane_iota, value[k : k + 1], 0)
        for step in range(PLANES):
            rows = slice(step * plane_rows, (step + 1) * plane_rows)
            tally = (jnp.right_shift(words, 8 * step) & 255).astype(F32)
            if (chunk + 1) * LANES <= atoms:
                kind = jnp.broadcast_to(species_cols[rows, 0:1], (plane_rows, LANES))
            else:
                kind = jnp.where(lane_block < ghosts, species_cols[rows, 1:2], species_cols[rows, 2:3])
            for s in range(species_count):
                count_ref[s, rows, lanes] = jnp.where(kind == float(s), tally, 0.0)

    hidden = jnp.zeros((channels, extent), F32)
    for s in range(species_count):
        hidden = hidden + embed_cols_ref[:, s : s + 1] * (species_f[0:1] == float(s)).astype(F32)
    hidden_ref[...] = hidden


def force_kernel(
    recv_ref, count_ref, hidden_ref, first_ref, first_t_ref, msg_t_ref, upd_t_ref, fan_ref, radial_ref, msg_ref, upd_ref, out_w_ref,
    out_ref,
    near_ref, inverse_ref, high_ref, low_ref, sums_ref, edge_ref, slope_pair_ref, slope_ref, row_h_ref, wide_ref, wave_ref,
    *, domains, slots, ghosts, reduced_dev,
):
    groups = recv_ref.shape[0] // domains
    rows = reduced_dev * 3
    pad_rows = -(-rows // 8) * 8
    atoms = recv_ref.shape[2] // 3
    extent = atoms + 2 * ghosts
    tail = atoms - ghosts
    species_count = count_ref.shape[0]
    basis_count, channels = radial_ref.shape
    own_chunks = atoms // LANES
    chunks = extent // LANES
    beads = range(reduced_dev)
    domain = lax.axis_index("space")
    scale = slots ** (-0.5)
    centers = [kappa * radial_reach * b / (basis_count - 1) for b in range(basis_count)]

    is_first = lax.broadcasted_iota(jnp.int32, (pad_rows, atoms), 0) < reduced_dev
    segment = {}
    for step in range(-2, 3):
        shifted = domain + step + 2 * domains
        place = lax.rem(shifted, domains)
        wraps = (lax.div(shifted, domains) - 2).astype(F32) * float(domains)
        total = recv_ref[place]
        for group in range(1, groups):
            total = total + recv_ref[group * domains + place]
        total = [total[:, x * atoms : (x + 1) * atoms] for x in range(3)]
        if rows < pad_rows:
            total.append(jnp.zeros((pad_rows - rows, atoms), F32))
        total = jnp.concatenate(total, axis=0)
        segment[step] = total + jnp.where(is_first, wraps, 0.0)

    def extended(step):
        return jnp.concatenate(
            [segment[step], segment[step - 1][:, tail:], segment[step + 1][:, :ghosts]], axis=1
        )

    ext_own, ext_left, ext_right = extended(0), extended(-1), extended(1)
    stacked = jnp.concatenate([ext_own, ext_left, ext_right], axis=0)
    high = stacked.astype(BF16).astype(F32)
    middle = (stacked - high).astype(BF16).astype(F32)
    parts = jnp.concatenate([high, middle, stacked - high - middle], axis=0)
    near_ref[...] = fast_dot(parts.T.astype(BF16), fan_ref[...])

    def near(own, q, at):
        start = (2 * q + (0 if own else 1)) * LANES
        return near_ref[at, start : start + LANES]


    for bead in beads:
        for chunk in range(chunks):
            lanes = slice(chunk * LANES, (chunk + 1) * LANES)
            own = chunk < own_chunks
            here = [
                jnp.broadcast_to(ext_own[x * reduced_dev + bead : x * reduced_dev + bead + 1, lanes], (ROWS, LANES))
                for x in range(3)
            ]

            def gather_basis(step, sums, bead=bead, lanes=lanes, own=own, here=here):
                at = pl.ds(pl.multiple_of(step * ROWS, ROWS), ROWS)
                square = spacing_floor
                for x in range(3):
                    delta = near(own, x * reduced_dev + bead, at) - here[x]
                    square = square + delta * delta
                inverse = lax.rsqrt(square)
                reach = square * inverse * kappa
                inverse_ref[bead, at, lanes] = inverse
                tallies = [count_ref[s, at, lanes] for s in range(species_count)]
                tally = functools.reduce(jnp.add, tallies)
                sums = list(sums)
                for b in range(basis_count):
                    offset = reach - centers[b]
                    value = jnp.exp2(-(offset * offset))
                    wave_ref[bead, b, at, lanes] = value * offset
                    for s in range(species_count):
                        term = tallies[s] * value
                        sums[b * species_count + s] = sums[b * species_count + s] + (term[:8] + term[8:])
                    if own:
                        high, low = halves(tally * value)
                        high_ref[bead, b, at, lanes] = high
                        low_ref[bead, b, at, lanes] = low
                return tuple(sums)

            zero = jnp.zeros((8, LANES), F32)
            sums = lax.fori_loop(0, extent // ROWS, gather_basis, (zero,) * (basis_count * species_count), unroll=UNROLL)
            for n, total in enumerate(sums):
                start = bead * extent + chunk * LANES
                sums_ref[n * 8 : n * 8 + 8, start : start + LANES] = total

    update = near_dot(first_t_ref[...], sums_ref[...])
    sigmoid = jax.nn.sigmoid(update)
    slope_ref[...] = sigmoid * (1.0 + update * (1.0 - sigmoid))
    hidden = jnp.concatenate([hidden_ref[...]] * reduced_dev, axis=1) + update * sigmoid
    lent_t = near_dot(msg_t_ref[...], hidden)
    lent = lent_t.T
    radial_cols = radial_ref[...].T * scale
    messages = []
    for bead in beads:
        for b in range(basis_count):
            high, low = halves(lent_t[:, bead * extent : (bead + 1) * extent] * radial_cols[:, b : b + 1])
            wide_ref[:channels, b * extent : (b + 1) * extent] = high
            wide_ref[channels:, b * extent : (b + 1) * extent] = low
        both = fast_dot(wide_ref[...], high_ref[bead].reshape(basis_count * extent, atoms))
        last = fast_dot(wide_ref[:channels], low_ref[bead].reshape(basis_count * extent, atoms))
        messages.append(both[:channels] + both[channels:] + last)
    message = jnp.concatenate(messages, axis=1)
    update = near_dot(upd_t_ref[...], message)
    sigmoid = jax.nn.sigmoid(update)
    out_cols = jnp.broadcast_to(out_w_ref[...], (8, channels)).T[:, 0:1]
    grad_update = out_cols * (sigmoid * (1.0 + update * (1.0 - sigmoid)))
    grad_message_t = near_dot(upd_ref[...], grad_update)
    grad_message = grad_message_t.T

    grads_lent = []
    for bead in beads:
        grad_lent = jnp.zeros((extent, channels), F32)
        for b in range(basis_count):
            high, low = halves(grad_message[bead * atoms : (bead + 1) * atoms] * (radial_ref[b : b + 1] * scale))
            both = fast_dot(high_ref[bead, b], jnp.concatenate([high, low], axis=1))
            grad_lent = grad_lent + both[:, :channels] + both[:, channels:] + fast_dot(low_ref[bead, b], high)
        grads_lent.append(grad_lent)
    grad_hidden = near_dot(msg_ref[...], jnp.concatenate(grads_lent, axis=0).T)
    parts = []
    for bead in beads:
        start = bead * extent
        parts += [grad_hidden[:, start : start + atoms] + out_cols, grad_hidden[:, start + atoms : start + extent]]
    row_h_ref[...] = near_dot(first_ref[...], jnp.concatenate(parts, axis=1) * slope_ref[...])
    for bead in beads:
        high, low = halves(grad_message_t[:, bead * atoms : (bead + 1) * atoms])
        grads = jnp.concatenate([high, high, low], axis=0)
        for b in range(basis_count):
            high, low = halves(lent[bead * extent : (bead + 1) * extent] * (radial_ref[b : b + 1] * scale))
            slope_pair_ref[bead, b] = fast_dot(jnp.concatenate([high, low, high], axis=1), grads)

    pulls = []
    edge_ref[...] = jnp.zeros_like(edge_ref)
    lane_row = lax.broadcasted_iota(jnp.int32, (BLOCK, LANES), 1)
    chain = -2.0 / (radial_width * math.sqrt(math.log2(math.e)))
    for bead in beads:
        for own in (True, False):
            lanes = slice(0, atoms) if own else slice(atoms, extent)
            width = atoms if own else extent - atoms
            start = bead * extent + lanes.start
            here = [ext_own[x * reduced_dev + bead : x * reduced_dev + bead + 1, lanes] for x in range(3)]

            def pair_grads(step, center, bead=bead, lanes=lanes, own=own, width=width, here=here, start=start):
                at = pl.ds(pl.multiple_of(step * BLOCK, BLOCK), BLOCK)
                tallies = [count_ref[s, at, lanes] for s in range(species_count)]
                total = jnp.zeros((BLOCK, width), F32)
                for b in range(basis_count):
                    value = wave_ref[bead, b, at, lanes]

                    def first_layer(s):
                        n = (b * species_count + s) * 8
                        tile = row_h_ref[n : n + 8, start : start + width]
                        return jnp.concatenate([tile] * (BLOCK // 8), axis=0)

                    slope = first_layer(0)
                    for s in range(1, species_count):
                        slope = jnp.where(tallies[s] > 0.0, first_layer(s), slope)
                    if own:
                        slope = slope + slope_pair_ref[bead, b, at, :]
                    total = total + slope * value
                weight = total * functools.reduce(jnp.add, tallies) * inverse_ref[bead, at, lanes] * chain
                center = list(center)
                columns = jnp.zeros((BLOCK, LANES), F32)
                for x in range(3):
                    q = x * reduced_dev + bead
                    place = near(own, q, at)
                    folded = None
                    for chunk in range(width // LANES):
                        cut = slice(chunk * LANES, (chunk + 1) * LANES)
                        pull = weight[:, cut] * (place - here[x][:, cut])
                        folded = pull if folded is None else folded + pull
                        n = x * (width // LANES) + chunk
                        for part in range(BLOCK // 8):
                            center[n] = center[n] + pull[part * 8 : part * 8 + 8]
                    if own:
                        columns = jnp.where(lane_row == q, jnp.sum(folded, axis=1, keepdims=True), columns)
                    else:
                        left = jnp.sum(jnp.where(lane_row < ghosts, folded, 0.0), axis=1, keepdims=True)
                        right = jnp.sum(jnp.where(lane_row < ghosts, 0.0, folded), axis=1, keepdims=True)
                        columns = jnp.where(lane_row == pad_rows + q, left, columns)
                        columns = jnp.where(lane_row == 2 * pad_rows + q, right, columns)
                edge_ref[at, :] = edge_ref[at, :] + columns
                return tuple(center)

            zero = jnp.zeros((8, LANES), F32)
            many = width // LANES
            center = lax.fori_loop(0, extent // BLOCK, pair_grads, (zero,) * (3 * many), unroll=extent // BLOCK)
            pulls.append(
                [
                    jnp.concatenate(
                        [jnp.sum(c, axis=0, keepdims=True) for c in center[x * many : (x + 1) * many]], axis=1
                    )
                    for x in range(3)
                ]
            )

    edges = edge_ref[...].T
    edge_own, edge_left, edge_right = (edges[pad_rows * n : pad_rows * (n + 1)] for n in range(3))
    center = [
        jnp.concatenate([pulls[2 * bead][x], pulls[2 * bead + 1][x]], axis=1) for x in range(3) for bead in beads
    ]
    if rows < pad_rows:
        center.append(jnp.zeros((pad_rows - rows, extent), F32))
    edge_own = edge_own - jnp.concatenate(center, axis=0)

    def at_head(values):
        return jnp.concatenate([values, jnp.zeros((pad_rows, tail), F32)], axis=1)

    def at_tail(values):
        return jnp.concatenate([jnp.zeros((pad_rows, tail), F32), values], axis=1)

    lower = slice(atoms, atoms + ghosts)
    upper = slice(atoms + ghosts, extent)
    back = {
        0: edge_own[:, :atoms] + at_head(edge_left[:, upper]) + at_tail(edge_right[:, lower]),
        -1: edge_left[:, :atoms] + at_tail(edge_own[:, lower]),
        1: edge_right[:, :atoms] + at_head(edge_own[:, upper]),
        -2: at_tail(edge_left[:, lower]),
        2: at_head(edge_right[:, upper]),
    }
    out_ref[0] = jnp.zeros_like(out_ref[0])
    for step, values in back.items():
        place = lax.rem(domain + step + 2 * domains, domains)
        flat = [values[x * reduced_dev : (x + 1) * reduced_dev] for x in range(3)]
        out_ref[0, place] = out_ref[0, place] + jnp.concatenate(flat, axis=1)
    for group in range(1, groups):
        out_ref[group] = out_ref[0]


def on_device(
    positions, species, neighbors, counts, send_rows, embed, w_radial, w_msg, w_upd, w_out
):
    full_dev, _, atoms = positions.shape
    groups = lax.axis_size("bead")
    domains = lax.axis_size("space")
    beads_all = full_dev * groups
    reduced_dev = PC // groups
    rows = -(-reduced_dev * 3 // 8) * 8
    slots = neighbors.shape[0]
    ghosts = send_rows.shape[0] // 2
    extent = atoms + 2 * ghosts
    species_count, channels = embed.shape
    layers, basis_count, _ = w_radial.shape
    back_table = collect_table(beads_all, groups)
    vmem = pl.BlockSpec(memory_space=pltpu.VMEM)
    params = pltpu.CompilerParams(vmem_limit_bytes=VMEM_BYTES)

    def shaped(*shape):
        return jax.ShapeDtypeStruct(shape, F32)

    sends = jnp.pad(send_rows, (0, atoms - 2 * ghosts))
    pack = jnp.concatenate([neighbors, counts[None], species[None], sends[None]], axis=0)

    def shift(values, by):
        return lax.ppermute(values, "space", [(i, (i + by) % domains) for i in range(domains)])

    from_left = shift(pack, 1)
    from_right = shift(pack, -1)
    from_far_left = shift(pack, 2)
    from_far_right = from_far_left if domains == 4 else shift(pack, -2)

    spread = pl.pallas_call(
        spread_kernel,
        out_shape=shaped(groups, domains, reduced_dev, 3 * atoms),
        in_specs=[vmem],
        out_specs=vmem,
        compiler_params=params,
    )(positions.transpose(1, 0, 2))
    arrived = lax.all_to_all(
        spread.reshape(groups * domains, reduced_dev, 3 * atoms), ("bead", "space"), 0, 0, tiled=True
    )

    sums_rows = basis_count * species_count * 8
    lane_count = 2 * LANES * 3 * reduced_dev
    embed_cols, *weights = pl.pallas_call(
        functools.partial(weights_kernel, slots=slots, ghosts=ghosts),
        out_shape=[
            shaped(channels, 8),
            shaped(sums_rows, channels),
            shaped(channels, sums_rows),
            shaped(channels, channels),
            shaped(channels, channels),
            jax.ShapeDtypeStruct((9 * rows, lane_count), BF16),
            shaped(basis_count, channels),
            shaped(channels, channels),
            shaped(channels, channels),
        ],
        in_specs=[vmem] * 4,
        out_specs=[vmem] * 9,
        compiler_params=params,
    )(embed, w_radial, w_msg, w_upd)
    prepared = pl.pallas_call(
        functools.partial(counts_kernel, slots=slots, ghosts=ghosts),
        out_shape=[shaped(species_count, extent, extent), shaped(channels, extent)],
        in_specs=[vmem] * 6,
        out_specs=[vmem] * 2,
        compiler_params=params,
    )(pack, from_left, from_right, from_far_left, from_far_right, embed_cols)

    grads = pl.pallas_call(
        functools.partial(force_kernel, domains=domains, slots=slots, ghosts=ghosts, reduced_dev=reduced_dev),
        out_shape=shaped(groups, domains, reduced_dev, 3 * atoms),
        in_specs=[vmem] * 12,
        out_specs=vmem,
        scratch_shapes=[
            pltpu.VMEM((extent, lane_count), F32),
            pltpu.VMEM((reduced_dev, extent, extent), F32),
            pltpu.VMEM((reduced_dev, basis_count, extent, atoms), BF16),
            pltpu.VMEM((reduced_dev, basis_count, extent, atoms), BF16),
            pltpu.VMEM((sums_rows, reduced_dev * extent), F32),
            pltpu.VMEM((extent, LANES), F32),
            pltpu.VMEM((reduced_dev, basis_count, extent, atoms), F32),
            pltpu.VMEM((channels, reduced_dev * extent), F32),
            pltpu.VMEM((sums_rows, reduced_dev * extent), F32),
            pltpu.VMEM((2 * channels, basis_count * extent), BF16),
            pltpu.VMEM((reduced_dev, basis_count, extent, extent), F32),
        ],
        compiler_params=params,
    )(arrived, *prepared, *weights, w_out[None])

    returned = lax.all_to_all(
        grads.reshape(groups * domains, reduced_dev, 3 * atoms), ("bead", "space"), 0, 0, tiled=True
    )
    forces = pl.pallas_call(
        collect_kernel,
        out_shape=shaped(3, full_dev, atoms),
        in_specs=[vmem, vmem],
        out_specs=vmem,
        compiler_params=params,
    )(back_table, returned.reshape(groups, domains, reduced_dev, 3 * atoms))
    return forces.transpose(1, 0, 2)


def solution(mesh):
    return jax.shard_map(
        on_device,
        mesh=mesh,
        in_specs=(
            P("bead", None, "space"),
            P("space"),
            P(None, "space"),
            P("space"),
            P("space"),
            P(),
            P(),
            P(),
            P(),
            P(),
        ),
        out_specs=P("bead", None, "space"),
        check_vma=False,
    )
```
